32 devices in a mesh: grp: 4 (over y, x), tile: 8 (over z, core).
Axes of the slice: x: 2, y: 2, z: 4, core: 2. Of those that a mesh axis runs over, the one named last changes fastest.
Arguments:
- adjoint_in: float32 [32768, 128], P(('grp', 'tile')), may hold values from -6 to 6
- departure: int32 [2, 32768], P(None, ('grp', 'tile')), may hold values from 0 to 32767, as said below
- fraction: float32 [2, 32768], P(None, ('grp', 'tile')), may hold values from 0 to 1
- level_map: float32 [2, 128, 128], replicated, may hold values from -0.5 to 0.5
- coarse_map: float32 [128, 4, 4], replicated, may hold values from -3 to 3
Outputs:
- adjoint_out: float32 [32768, 128], P(('grp', 'tile'))
The draws below stay inside these ranges and needn't reach their ends.
Inputs may be any that keep to these rules, and one draw needn't show every extreme that they name: For each step, the departure cell of a column lies in the same block row, on the device whose tile index differs from the column's own by at most 2, counted periodically along tile. Of the columns of one device, at most 512 have departure cells on any one device, and on every device exactly 512 of them share one device.
All inputs are finite; a program needn't handle non-finite values.
Results may differ from the reference program's by a relative error of at most 0.00013.
Values sent between devices are 32-bit elements; how exact they have to be, the bound alone decides.
A program may use at most 64 MiB of HBM per device.

```python
import jax
import jax.numpy as jnp
from jax import lax

LEV = 128
COLS_DEV = 1024
REACH = 2
NCOLS = 32768
N_GRP = 4
N_TILE = 8


def draw_departure(key, part):
    devices_all = N_GRP * N_TILE
    width_span = 2 * REACH + 1
    key_wind, key_order, key_other, key_place = jax.random.split(key, 4)
    wind = jax.random.randint(key_wind, (2, devices_all, 1), -REACH, REACH + 1)
    scores = jax.random.randint(key_order, (2, devices_all, COLS_DEV), 0, 2 ** 18) * COLS_DEV + jnp.arange(COLS_DEV, dtype=jnp.int32)
    ranking = jnp.argsort(jnp.argsort(scores, axis=-1), axis=-1)
    leading = ranking < COLS_DEV // 2
    stride = jax.random.randint(key_other, (2, devices_all, COLS_DEV), 1, width_span)
    other = (wind + REACH + stride) % width_span - REACH
    offset = jnp.where(leading, wind, other)
    device_ids = jnp.arange(devices_all, dtype=jnp.int32)
    group_ids = device_ids // N_TILE
    tile_ids = device_ids % N_TILE
    target_tile = (tile_ids[None, :, None] + offset) % N_TILE
    place = jax.random.randint(key_place, (2, devices_all, COLS_DEV), 0, COLS_DEV)
    result = (group_ids[None, :, None] * N_TILE + target_tile) * COLS_DEV + place
    return result.reshape(2, devices_all * COLS_DEV).astype(jnp.int32)


def block_scale(own_key, extent, shards, low, largest):
    level, own = 1.0, jax.random.fold_in(own_key, 6)
    for dim, shards_of in shards:
        draws = jnp.exp(jax.random.uniform(jax.random.fold_in(own, dim), (shards_of,), jnp.float32, low / len(shards), largest / len(shards)))
        level = level * jnp.repeat(draws, extent[dim] // shards_of).reshape([-1 if axis == dim else 1 for axis in range(len(extent))])
    return level


def noise(own_key, shape, width, limit, shards=(), held_as=jnp.bfloat16):
    drawn = width * jax.random.normal(own_key, shape, jnp.float32)
    if shards:
        drawn = drawn * block_scale(own_key, shape, shards, -0.22, 0.18)
    return jnp.clip(drawn, -limit, limit).astype(held_as)


def setup_inputs(seed: int = 0) -> dict:
    key_of = jax.random.split(jax.random.key(seed), 6)
    return {
        "adjoint_in": noise(key_of[0], (NCOLS, LEV), 1.0, 6.0, ((0, 32),), jnp.float32),
        "departure": draw_departure(jax.random.fold_in(key_of[5], 71), 0),
        "fraction": jnp.clip(1.0 * jax.random.uniform(key_of[2], (2, NCOLS), jnp.float32) ** block_scale(key_of[2], (2, NCOLS), ((1, 32),), -0.2, 0.2), 0.0, 1.0),
        "level_map": noise(key_of[3], (2, LEV, LEV), LEV ** -0.5, 0.5, (), jnp.float32),
        "coarse_map": noise(key_of[4], (LEV, N_GRP, N_GRP), N_GRP ** -0.5, 3.0, (), jnp.float32),
    }


def cubic_weights(fraction):
    alpha = fraction
    return [-alpha * (1.0 - alpha) * (2.0 - alpha) / 6.0,
            (1.0 + alpha) * (1.0 - alpha) * (2.0 - alpha) / 2.0,
            (1.0 + alpha) * alpha * (2.0 - alpha) / 2.0,
            -(1.0 + alpha) * alpha * (1.0 - alpha) / 6.0]


def transport_adjoint(field, departure, fraction, level_map):
    lifted = jnp.dot(field, level_map.T, precision=lax.Precision.HIGHEST, preferred_element_type=jnp.float32)
    row_span = COLS_DEV * N_TILE
    row_start = (departure // row_span) * row_span
    result = jnp.zeros_like(lifted)
    for stencil, weight in enumerate(cubic_weights(fraction)):
        target = row_start + (departure - row_start + stencil - 1) % row_span
        result = result.at[target].add(weight[:, None] * lifted)
    return result


def couple_rows(field, coarse_map):
    blocks = field.reshape(N_GRP, COLS_DEV * N_TILE, LEV)
    mixed = jnp.einsum("ecl,lbe->bcl", blocks, coarse_map, precision=lax.Precision.HIGHEST)
    return mixed.reshape(N_GRP * COLS_DEV * N_TILE, LEV)


def reference(adjoint_in, departure, fraction, level_map, coarse_map):
    second = transport_adjoint(adjoint_in, departure[1], fraction[1], level_map[1])
    coupled = couple_rows(second, coarse_map)
    return transport_adjoint(coupled, departure[0], fraction[0], level_map[0])
```

```python
import functools

import jax
import jax.numpy as jnp
from jax import lax
from jax.experimental import pallas as pl
from jax.experimental.pallas import tpu as pltpu
from jax.sharding import PartitionSpec as P

REACH = 2
SHIFTS = (2, -2, 1, -1, 0)
REMOTE = 4
BF16 = jnp.bfloat16
F32 = jnp.float32


def cubic_weights(a):
    return [
        -a * (1.0 - a) * (2.0 - a) / 6.0,
        (1.0 + a) * (1.0 - a) * (2.0 - a) / 2.0,
        (1.0 + a) * a * (2.0 - a) / 2.0,
        -(1.0 + a) * a * (1.0 - a) / 6.0,
    ]


def split(x):
    high = x.astype(BF16)
    return high, (x - high.astype(F32)).astype(BF16)


def dot(a, b):
    return jnp.dot(a, b, preferred_element_type=F32)


def dot_nt(a, b):
    return lax.dot_general(a, b, (((1,), (1,)), ((), ())), preferred_element_type=F32)


def kernel(
    n_grp, n_tile, x_ref, meta_ref, lm_ref, cm_ref, out_ref,
    tri, slots, pick, lifted, rows_out, rows_in, meta_out, meta_in, rows_hl,
    land, edge, edge_in, field, grp_in, grp_mid, grp_last,
    rows_ss, rows_rs, meta_ss, meta_rs, edge_ss, edge_rs, grp_ss, grp_rs,
):
    cols = x_ref.shape[0]
    lev = x_ref.shape[1]
    half = cols // 2
    grp = lax.axis_index("grp")
    tile = lax.axis_index("tile")

    def at_tile(by):
        return {"tile": lax.rem(tile + (by + n_tile), n_tile)}

    def at_grp(g):
        return {"grp": g}

    barrier = pltpu.get_barrier_semaphore()
    for by in SHIFTS[:REMOTE]:
        pl.semaphore_signal(barrier, inc=1, device_id=at_tile(by), device_id_type=pl.DeviceIdType.MESH)
    for step in range(1, n_grp):
        pl.semaphore_signal(
            barrier, inc=1, device_id=at_grp(lax.rem(grp + step, n_grp)),
            device_id_type=pl.DeviceIdType.MESH,
        )
    pl.semaphore_wait(barrier, REMOTE + n_grp - 1)

    sent = []
    metas = ([], [])

    def send(src, dst, ss, rs, where):
        copy = pltpu.make_async_remote_copy(
            src_ref=src, dst_ref=dst, send_sem=ss, recv_sem=rs,
            device_id=where, device_id_type=pl.DeviceIdType.MESH,
        )
        copy.start()
        sent.append(copy)
        return copy

    block = 128

    @pl.loop(0, cols // block)
    def _(i):
        r = lax.broadcasted_iota(jnp.int32, (block, cols), 0) + i * block
        c = lax.broadcasted_iota(jnp.int32, (block, cols), 1)
        tri[pl.ds(pl.multiple_of(i * block, block), block), :] = jnp.where(r < c, 1.0, 0.0).astype(BF16)

    row8 = lax.broadcasted_iota(jnp.int32, (8, cols), 0)
    wanted = jnp.full((8, cols), -100.0, F32)
    for j, by in enumerate(SHIFTS):
        wanted = jnp.where(row8 == j, float(by), wanted)
    hot = jnp.concatenate([wanted == meta_ref[1, 5:6, :], wanted == meta_ref[0, 5:6, :]], axis=0)
    before = dot(jnp.where(hot, 1.0, 0.0).astype(BF16), tri[...])
    slots[...] = jnp.where(hot, before, -1.0).astype(jnp.int32)

    def build_pick(t, j):
        @pl.loop(0, half // block)
        def _(i):
            r = lax.broadcasted_iota(jnp.int32, (block, cols), 0) + i * block
            hit = r == slots[8 * t + j : 8 * t + j + 1, :]
            pick[t, j, pl.ds(pl.multiple_of(i * block, block), block), :] = jnp.where(hit, 1.0, 0.0).astype(BF16)

    def pack_meta(t, j):
        whole = meta_ref[1 - t]
        a = whole.astype(BF16)
        rest = whole - a.astype(F32)
        b = rest.astype(BF16)
        parts = jnp.concatenate([a.astype(F32), b.astype(F32)], axis=0).astype(BF16)
        got = dot_nt(parts, pick[t, j])
        return got[:8] + got[8:]

    def do_meta(t):
        for j in range(REMOTE):
            meta_out[t, j] = pack_meta(t, j)
            metas[t].append(
                send(meta_out.at[t, j], meta_in.at[t, j], meta_ss.at[t, j], meta_rs.at[t, j], at_tile(SHIFTS[j]))
            )
        meta_in[t, REMOTE] = pack_meta(t, REMOTE)

    def spread(cells, parcel):
        place = parcel[0:1].astype(jnp.int32)
        result = jnp.zeros(cells.shape, F32)
        for k in range(4):
            result = jnp.where(cells == place + (k - 1), parcel[1 + k : 2 + k], result)
        return split(result)

    def product(s_high, s_low):
        wide = dot(s_high, rows_hl[...])
        return wide[:, :lev] + wide[:, lev:] + dot(s_low, rows_hl[:, :lev])

    def edge_part(t, j):
        high, low = split(rows_in[t, j])
        rows_hl[:, :lev] = high
        rows_hl[:, lev:] = low
        r = lax.broadcasted_iota(jnp.int32, (16, half), 0)
        cells = jnp.where(r == 0, -1, jnp.where(r <= 2, cols - 1 + r, -100))
        return product(*spread(cells, meta_in[t, j]))[:8]

    def deposit(t, j, first):
        size = 256

        @pl.loop(0, cols // size)
        def _(i):
            cells = lax.broadcasted_iota(jnp.int32, (size, half), 0) + i * size
            part = product(*spread(cells, meta_in[t, j]))
            at = pl.ds(pl.multiple_of(i * size, size), size)
            if first:
                land[t, at, :] = part
            else:
                land[t, at, :] += part

    def transport(t, src):
        m_high, m_low = split(lm_ref[1 - t])
        f_high, f_low = split(src[...])
        lift = dot_nt(f_high, m_high) + dot_nt(f_low, m_high) + dot_nt(f_high, m_low)
        l_high, l_low = split(lift)
        lifted[:, :lev] = l_high
        lifted[:, lev:] = l_low
        copies = []
        for j in range(REMOTE + 1):
            if t == 0:
                build_pick(t, j)
            both = dot(pick[t, j], lifted[...])
            packed = both[:, :lev] + both[:, lev:]
            if j < REMOTE:
                rows_out[t, j] = packed
                copies.append(
                    send(rows_out.at[t, j], rows_in.at[t, j], rows_ss.at[t, j], rows_rs.at[t, j], at_tile(SHIFTS[j]))
                )
            else:
                rows_in[t, j] = packed
        if t == 0:
            do_meta(0)
        border = edge_part(t, REMOTE)
        deposit(t, REMOTE, True)
        if t == 0:
            for j in range(REMOTE + 1):
                build_pick(1, j)
            do_meta(1)
        for n, j in enumerate((2, 3, 0, 1)):
            copies[j].wait_recv()
            metas[t][j].wait_recv()
            border = border + edge_part(t, j)
            if n == REMOTE - 1:
                edge[t] = border
                to_next = send(edge.at[t], edge_in.at[t, 0], edge_ss.at[t, 0], edge_rs.at[t, 0], at_tile(1))
                to_prev = send(edge.at[t], edge_in.at[t, 1], edge_ss.at[t, 1], edge_rs.at[t, 1], at_tile(-1))
            deposit(t, j, False)
        to_next.wait_recv()
        to_prev.wait_recv()
        r = lax.broadcasted_iota(jnp.int32, (8, lev), 0)
        from_prev = edge_in[t, 0]
        from_next = edge_in[t, 1]
        land[t, 0:8, :] += jnp.where(r == 0, from_prev[1:2], jnp.where(r == 1, from_prev[2:3], 0.0))
        land[t, cols - 8 : cols, :] += jnp.where(r == 7, from_next[0:1], 0.0)

    def coarse(b, e):
        return cm_ref[b, pl.ds(e, 1), :]

    transport(0, x_ref)

    if n_grp == 4:
        flip_x = grp + 1 - 2 * lax.rem(grp, 2)
        flip_y = lax.rem(grp + 2, 4)
        orders = ((flip_x, flip_y), (flip_y, flip_x))
        firsts = []
        lasts = []
        for h, (near, far) in enumerate(orders):
            at = pl.ds(h * half, half)
            firsts.append(send(land.at[0, at], grp_in.at[0, at], grp_ss.at[0, h], grp_rs.at[0, h], at_grp(near)))
        for h, (near, far) in enumerate(orders):
            at = pl.ds(h * half, half)
            firsts[h].wait_recv()
            grp_mid[at, :] = coarse(far, grp) * land[0, at, :] + coarse(far, near) * grp_in[0, at, :]
            lasts.append(send(grp_mid.at[at], grp_last.at[at], grp_ss.at[1, h], grp_rs.at[1, h], at_grp(far)))
        for h, (near, far) in enumerate(orders):
            at = pl.ds(h * half, half)
            field[at, :] = coarse(grp, grp) * land[0, at, :] + coarse(grp, near) * grp_in[0, at, :]
        for h in range(2):
            at = pl.ds(h * half, half)
            lasts[h].wait_recv()
            field[at, :] += grp_last[at, :]
    else:
        copies = []
        for step in range(1, n_grp):
            to = lax.rem(grp + step, n_grp)
            copies.append(
                send(land.at[0], grp_in.at[step - 1], grp_ss.at[step - 1, 0], grp_rs.at[step - 1, 0], at_grp(to))
            )
        field[...] = coarse(grp, grp) * land[0]
        for step in range(1, n_grp):
            copies[step - 1].wait_recv()
            field[...] += coarse(grp, lax.rem(grp + n_grp - step, n_grp)) * grp_in[step - 1]

    transport(1, field)
    out_ref[...] = land[1]
    for copy in sent:
        copy.wait_send()


def body(n_grp, n_tile, adjoint_in, departure, fraction, level_map, coarse_map):
    cols, lev = adjoint_in.shape
    half = cols // 2
    tile_self = lax.axis_index("tile")
    places = (departure % cols).astype(F32)
    offset = (departure // cols % n_tile - tile_self + REACH) % n_tile - REACH
    blank = jnp.zeros_like(places)
    meta = jnp.stack([places] + cubic_weights(fraction) + [offset.astype(F32), blank, blank], axis=1)
    vmem = pl.BlockSpec(memory_space=pltpu.VMEM)
    n_in = 1 if n_grp == 4 else n_grp - 1
    dma = pltpu.SemaphoreType.DMA
    return pl.pallas_call(
        functools.partial(kernel, n_grp, n_tile),
        out_shape=jax.ShapeDtypeStruct((cols, lev), F32),
        in_specs=[vmem] * 4,
        out_specs=vmem,
        scratch_shapes=[
            pltpu.VMEM((cols, cols), BF16),
            pltpu.VMEM((16, cols), jnp.int32),
            pltpu.VMEM((2, REMOTE + 1, half, cols), BF16),
            pltpu.VMEM((cols, 2 * lev), BF16),
            pltpu.VMEM((2, REMOTE, half, lev), F32),
            pltpu.VMEM((2, REMOTE + 1, half, lev), F32),
            pltpu.VMEM((2, REMOTE, 8, half), F32),
            pltpu.VMEM((2, REMOTE + 1, 8, half), F32),
            pltpu.VMEM((half, 2 * lev), BF16),
            pltpu.VMEM((2, cols, lev), F32),
            pltpu.VMEM((2, 8, lev), F32),
            pltpu.VMEM((2, 2, 8, lev), F32),
            pltpu.VMEM((cols, lev), F32),
            pltpu.VMEM((n_in, cols, lev), F32),
            pltpu.VMEM((cols, lev), F32),
            pltpu.VMEM((cols, lev), F32),
            dma((2, REMOTE)),
            dma((2, REMOTE)),
            dma((2, REMOTE)),
            dma((2, REMOTE)),
            dma((2, 2)),
            dma((2, 2)),
            dma((max(2, n_grp - 1), 2)),
            dma((max(2, n_grp - 1), 2)),
        ],
        compiler_params=pltpu.CompilerParams(
            collective_id=0, has_side_effects=True, vmem_limit_bytes=48 * 2 ** 20
        ),
    )(adjoint_in, meta, level_map, coarse_map.transpose(1, 2, 0))


def solution(mesh):
    return jax.shard_map(
        functools.partial(body, mesh.shape["grp"], mesh.shape["tile"]),
        mesh=mesh,
        in_specs=(
            P(("grp", "tile"), None),
            P(None, ("grp", "tile")),
            P(None, ("grp", "tile")),
            P(),
            P(),
        ),
        out_specs=P(("grp", "tile"), None),
        check_vma=False,
    )
```

```python
import functools

import jax
import jax.numpy as jnp
from jax import lax
from jax.experimental import pallas as pl
from jax.experimental.pallas import tpu as pltpu
from jax.sharding import PartitionSpec as P

REACH = 2
SHIFTS = (2, -2, 1, -1, 0)
REMOTE = 4
EDGE_SHIFTS = (1, -1, 2, -2, 3, -3)
CHUNKS = 4
BF16 = jnp.bfloat16
F32 = jnp.float32


def cubic_weights(a):
    return [
        -a * (1.0 - a) * (2.0 - a) / 6.0,
        (1.0 + a) * (1.0 - a) * (2.0 - a) / 2.0,
        (1.0 + a) * a * (2.0 - a) / 2.0,
        -(1.0 + a) * a * (1.0 - a) / 6.0,
    ]


def split(x):
    high = x.astype(BF16)
    return high, (x - high.astype(F32)).astype(BF16)


def dot(a, b):
    return jnp.dot(a, b, preferred_element_type=F32)


def dot_nt(a, b):
    return lax.dot_general(a, b, (((1,), (1,)), ((), ())), preferred_element_type=F32)


def kernel(
    n_grp, n_tile, x_hbm, lm_hbm, meta_ref, cm_ref, out_ref,
    x_ref, lm_ref, slots, pick, lifted, rows_out, rows_in, meta_out, meta_in, rows_hl,
    s_high, s_low, land, edge, edge_in, field, grp_in, grp_mid, grp_last,
    load_sem, rows_ss, rows_rs, meta_ss, meta_rs, edge_ss, edge_rs, grp_ss, grp_rs,
):
    cols, lev = x_ref.shape
    half = cols // 2
    grp = lax.axis_index("grp")
    tile = lax.axis_index("tile")

    def at_tile(by):
        return {"tile": lax.rem(tile + (by + n_tile), n_tile)}

    def at_grp(g):
        return {"grp": g}

    barrier = pltpu.get_barrier_semaphore()
    for by in EDGE_SHIFTS:
        pl.semaphore_signal(barrier, inc=1, device_id=at_tile(by), device_id_type=pl.DeviceIdType.MESH)
    for step in range(1, n_grp):
        pl.semaphore_signal(
            barrier, inc=1, device_id=at_grp(lax.rem(grp + step, n_grp)),
            device_id_type=pl.DeviceIdType.MESH,
        )
    loads = [
        pltpu.make_async_copy(x_hbm, x_ref, load_sem.at[0]),
        pltpu.make_async_copy(lm_hbm, lm_ref, load_sem.at[1]),
    ]
    for load in loads:
        load.start()

    sent = []
    metas = ([], [])

    def send(src, dst, ss, rs, where):
        copy = pltpu.make_async_remote_copy(
            src_ref=src, dst_ref=dst, send_sem=ss, recv_sem=rs,
            device_id=where, device_id_type=pl.DeviceIdType.MESH,
        )
        copy.start()
        sent.append(copy)
        return copy

    row8 = lax.broadcasted_iota(jnp.int32, (8, cols), 0)
    wanted = jnp.full((8, cols), -100.0, F32)
    for j, by in enumerate(SHIFTS):
        wanted = jnp.where(row8 == j, float(by), wanted)
    hot = jnp.concatenate(
        [jnp.where(wanted == meta_ref[1 - t, 5:6, :], 1.0, 0.0) for t in range(2)], axis=0
    )
    lane = 128
    r = lax.broadcasted_iota(jnp.int32, (lane, 2 * lane), 0)
    c = lax.broadcasted_iota(jnp.int32, (lane, 2 * lane), 1)
    counter = jnp.where((r < c) | (c >= lane), 1.0, 0.0).astype(BF16)
    stacked = jnp.concatenate([hot[:, i * lane : (i + 1) * lane] for i in range(cols // lane)], axis=0)
    counts = dot(stacked.astype(BF16), counter)
    total = jnp.zeros((16, lane), F32)
    for i in range(cols // lane):
        own = counts[16 * i : 16 * i + 16]
        before = own[:, :lane] + total
        total = total + own[:, lane:]
        mine = hot[:, i * lane : (i + 1) * lane] > 0.5
        slots[:, i * lane : (i + 1) * lane] = jnp.where(mine, before, -1.0).astype(jnp.int32)

    block = 128

    def build_pick(t, j):
        @pl.loop(0, half // block)
        def _(i):
            r = lax.broadcasted_iota(jnp.int32, (block, cols), 0) + i * block
            hit = r == slots[8 * t + j : 8 * t + j + 1, :]
            pick[t, j, pl.ds(pl.multiple_of(i * block, block), block), :] = jnp.where(hit, 1.0, 0.0).astype(BF16)

    def do_meta(t, j):
        whole = meta_ref[1 - t]
        a = whole.astype(BF16)
        rest = whole - a.astype(F32)
        parts = jnp.concatenate([a.astype(F32), rest], axis=0).astype(BF16)
        got = dot_nt(parts, pick[t, j])
        packed = got[:8] + got[8:]
        if j == REMOTE:
            meta_in[t, j] = packed
        else:
            meta_out[t, j] = packed
            metas[t].append(
                send(meta_out.at[t, j], meta_in.at[t, j], meta_ss.at[t, j], meta_rs.at[t, j], at_tile(SHIFTS[j]))
            )

    def build_spread(t, j):
        if j < REMOTE:
            metas[t][j].wait_recv()
        size = 128

        @pl.loop(0, cols // size)
        def _(i):
            cells = lax.broadcasted_iota(jnp.int32, (size, half), 0) + i * size
            place = meta_in[t, j, 0:1, :].astype(jnp.int32)
            value = jnp.zeros((size, half), F32)
            for k in range(4):
                value = jnp.where(cells == place + (k - 1), meta_in[t, j, 1 + k : 2 + k, :], value)
            high, low = split(value)
            at = pl.ds(pl.multiple_of(i * size, size), size)
            s_high[j, at, :] = high
            s_low[j, at, :] = low

    def deposit(t, j, first):
        high, low = split(rows_in[t, j])
        rows_hl[:, :lev] = high
        rows_hl[:, lev:] = low
        size = 512

        @pl.loop(0, cols // size)
        def _(i):
            at = pl.ds(pl.multiple_of(i * size, size), size)
            wide = dot(s_high[j, at, :], rows_hl[...])
            part = wide[:, :lev] + wide[:, lev:] + dot(s_low[j, at, :], rows_hl[:, :lev])
            if first:
                land[t, at, :] = part
            else:
                land[t, at, :] += part

    def send_edges(t):
        place = meta_ref[1 - t, 0:1, :]
        w = [meta_ref[1 - t, 1 + k : 2 + k, :] for k in range(4)]
        offset = meta_ref[1 - t, 5:6, :]
        last = place == float(cols - 1)
        forward = jnp.where(last, w[2], jnp.where(place == float(cols - 2), w[3], 0.0))
        forward2 = jnp.where(last, w[3], 0.0)
        backward = jnp.where(place == 0.0, w[0], 0.0)
        blocks = []
        for by in EDGE_SHIFTS + (0, 0):
            near = offset == float(by - 1)
            value = jnp.where(row8 == 0, jnp.where(near, forward, 0.0), 0.0)
            value = jnp.where(row8 == 1, jnp.where(near, forward2, 0.0), value)
            value = jnp.where(row8 == 2, jnp.where(offset == float(by + 1), backward, 0.0), value)
            blocks.append(value)
        high, low = split(jnp.concatenate(blocks, axis=0))
        wide = dot(high, lifted[...])
        sums = wide[:, :lev] + wide[:, lev:] + dot(low, lifted[:, :lev])
        copies = []
        for n, by in enumerate(EDGE_SHIFTS):
            edge[t, n] = sums[8 * n : 8 * n + 8]
            copies.append(send(edge.at[t, n], edge_in.at[t, n], edge_ss.at[t, n], edge_rs.at[t, n], at_tile(by)))
        n = len(EDGE_SHIFTS)
        edge[t, n] = sums[8 * n : 8 * n + 8]
        return copies

    def transport(t, src):
        m_high, m_low = split(lm_ref[1 - t])
        f_high, f_low = split(src[...])
        lift = dot_nt(f_high, m_high) + dot_nt(f_low, m_high) + dot_nt(f_high, m_low)
        l_high, l_low = split(lift)
        lifted[:, :lev] = l_high
        lifted[:, lev:] = l_low
        copies = []
        for j in range(REMOTE + 1):
            if t == 0:
                build_pick(t, j)
                if j == 0:
                    pl.semaphore_wait(barrier, len(EDGE_SHIFTS) + n_grp - 1)
                do_meta(t, j)
            both = dot(pick[t, j], lifted[...])
            packed = both[:, :lev] + both[:, lev:]
            if j < REMOTE:
                rows_out[t, j] = packed
                copies.append(
                    send(rows_out.at[t, j], rows_in.at[t, j], rows_ss.at[t, j], rows_rs.at[t, j], at_tile(SHIFTS[j]))
                )
            else:
                rows_in[t, j] = packed
        edges = send_edges(t)
        if t == 0:
            build_spread(t, REMOTE)
        deposit(t, REMOTE, True)
        if t == 0:
            for j in range(REMOTE):
                build_spread(t, j)
        for j in (2, 3, 0, 1):
            copies[j].wait_recv()
            deposit(t, j, False)
        sums = edge[t, len(edges)]
        for n, copy in enumerate(edges):
            copy.wait_recv()
            sums = sums + edge_in[t, n]
        r = lax.broadcasted_iota(jnp.int32, (8, lev), 0)
        land[t, 0:8, :] += jnp.where(r < 2, sums, 0.0)
        land[t, cols - 8 : cols, :] += jnp.where(r == 7, sums[2:3], 0.0)

    def prepare():
        for j in range(REMOTE + 1):
            build_pick(1, j)
            do_meta(1, j)

    def prepare_spread():
        for j in range(REMOTE + 1):
            build_spread(1, j)

    def coarse(b, e):
        return cm_ref[b, pl.ds(e, 1), :]

    for load in loads:
        load.wait()
    transport(0, x_ref)

    if n_grp == 4:
        flip_x = grp + 1 - 2 * lax.rem(grp, 2)
        flip_y = lax.rem(grp + 2, 4)
        chunks = []
        for n in range(CHUNKS):
            near, far = ((flip_x, flip_y), (flip_y, flip_x))[n % 2]
            chunks.append((n, pl.ds(n * (cols // CHUNKS), cols // CHUNKS), near, far))
        firsts = []
        lasts = []
        for n, at, near, far in chunks:
            firsts.append(send(land.at[0, at], grp_in.at[0, at], grp_ss.at[0, n], grp_rs.at[0, n], at_grp(near)))
        prepare()
        for n, at, near, far in chunks:
            firsts[n].wait_recv()
            grp_mid[at, :] = coarse(far, grp) * land[0, at, :] + coarse(far, near) * grp_in[0, at, :]
            lasts.append(send(grp_mid.at[at], grp_last.at[at], grp_ss.at[1, n], grp_rs.at[1, n], at_grp(far)))
        for n, at, near, far in chunks:
            field[at, :] = coarse(grp, grp) * land[0, at, :] + coarse(grp, near) * grp_in[0, at, :]
        prepare_spread()
        for n, at, near, far in chunks:
            lasts[n].wait_recv()
            field[at, :] += grp_last[at, :]
    else:
        copies = []
        for step in range(1, n_grp):
            to = lax.rem(grp + step, n_grp)
            copies.append(
                send(land.at[0], grp_in.at[step - 1], grp_ss.at[step - 1, 0], grp_rs.at[step - 1, 0], at_grp(to))
            )
        prepare()
        prepare_spread()
        field[...] = coarse(grp, grp) * land[0]
        for step in range(1, n_grp):
            copies[step - 1].wait_recv()
            field[...] += coarse(grp, lax.rem(grp + n_grp - step, n_grp)) * grp_in[step - 1]

    transport(1, field)
    out_ref[...] = land[1]
    for copy in sent:
        copy.wait_send()


def body(n_grp, n_tile, adjoint_in, departure, fraction, level_map, coarse_map):
    cols, lev = adjoint_in.shape
    half = cols // 2
    tile_self = lax.axis_index("tile")
    places = (departure % cols).astype(F32)
    offset = (departure // cols % n_tile - tile_self + REACH) % n_tile - REACH
    blank = jnp.zeros_like(places)
    meta = jnp.stack([places] + cubic_weights(fraction) + [offset.astype(F32), blank, blank], axis=1)
    vmem = pl.BlockSpec(memory_space=pltpu.VMEM)
    n_in = 1 if n_grp == 4 else n_grp - 1
    dma = pltpu.SemaphoreType.DMA
    return pl.pallas_call(
        functools.partial(kernel, n_grp, n_tile),
        out_shape=jax.ShapeDtypeStruct((cols, lev), F32),
        in_specs=[pl.BlockSpec(memory_space=pl.ANY)] * 2 + [vmem] * 2,
        out_specs=vmem,
        scratch_shapes=[
            pltpu.VMEM((cols, lev), F32),
            pltpu.VMEM(level_map.shape, F32),
            pltpu.VMEM((16, cols), jnp.int32),
            pltpu.VMEM((2, REMOTE + 1, half, cols), BF16),
            pltpu.VMEM((cols, 2 * lev), BF16),
            pltpu.VMEM((2, REMOTE, half, lev), F32),
            pltpu.VMEM((2, REMOTE + 1, half, lev), F32),
            pltpu.VMEM((2, REMOTE, 8, half), F32),
            pltpu.VMEM((2, REMOTE + 1, 8, half), F32),
            pltpu.VMEM((half, 2 * lev), BF16),
            pltpu.VMEM((REMOTE + 1, cols, half), BF16),
            pltpu.VMEM((REMOTE + 1, cols, half), BF16),
            pltpu.VMEM((2, cols, lev), F32),
            pltpu.VMEM((2, len(EDGE_SHIFTS) + 1, 8, lev), F32),
            pltpu.VMEM((2, len(EDGE_SHIFTS), 8, lev), F32),
            pltpu.VMEM((cols, lev), F32),
            pltpu.VMEM((n_in, cols, lev), F32),
            pltpu.VMEM((cols, lev), F32),
            pltpu.VMEM((cols, lev), F32),
            dma((2,)),
            dma((2, REMOTE)),
            dma((2, REMOTE)),
            dma((2, REMOTE)),
            dma((2, REMOTE)),
            dma((2, len(EDGE_SHIFTS))),
            dma((2, len(EDGE_SHIFTS))),
            dma((max(2, n_grp - 1), CHUNKS)),
            dma((max(2, n_grp - 1), CHUNKS)),
        ],
        compiler_params=pltpu.CompilerParams(
            collective_id=0, has_side_effects=True, vmem_limit_bytes=48 * 2 ** 20
        ),
    )(adjoint_in, level_map, meta, coarse_map.transpose(1, 2, 0))


def solution(mesh):
    return jax.shard_map(
        functools.partial(body, mesh.shape["grp"], mesh.shape["tile"]),
        mesh=mesh,
        in_specs=(
            P(("grp", "tile"), None),
            P(None, ("grp", "tile")),
            P(None, ("grp", "tile")),
            P(),
            P(),
        ),
        out_specs=P(("grp", "tile"), None),
        check_vma=False,
    )
```

```python
import functools

import jax
import jax.numpy as jnp
from jax import lax
from jax.experimental import pallas as pl
from jax.experimental.pallas import tpu as pltpu
from jax.sharding import PartitionSpec as P

REACH = 2
SHIFTS = (2, -2, 1, -1, 0)
REMOTE = 4
EDGE_SHIFTS = (1, -1, 2, -2, 3, -3)
CHUNKS = 4
ARRIVE = (2, 3, 0, 1)
BF16 = jnp.bfloat16
F32 = jnp.float32


def cubic_weights(a):
    return [
        -a * (1.0 - a) * (2.0 - a) / 6.0,
        (1.0 + a) * (1.0 - a) * (2.0 - a) / 2.0,
        (1.0 + a) * a * (2.0 - a) / 2.0,
        -(1.0 + a) * a * (1.0 - a) / 6.0,
    ]


def split(x):
    high = x.astype(BF16)
    return high, (x - high.astype(F32)).astype(BF16)


def dot(a, b):
    return jnp.dot(a, b, preferred_element_type=F32)


def dot_nt(a, b):
    return lax.dot_general(a, b, (((1,), (1,)), ((), ())), preferred_element_type=F32)


def kernel(
    n_grp, n_tile, x_hbm, dep_hbm, frac_hbm, lm_hbm, cm_hbm, out_ref,
    x_ref, dep_ref, frac_ref, lm_ref, cm_ref, meta_ref,
    slots, pick, lifted, rows_out, rows_in, meta_out, meta_in, rows_hl,
    s_high, s_low, land, edge, edge_in, field, grp_out, grp_in, grp_mid, grp_last,
    load_sem, rows_ss, rows_rs, meta_ss, meta_rs, edge_ss, edge_rs, grp_ss, grp_rs,
):
    cols, lev = x_ref.shape
    half = cols // 2
    grp = lax.axis_index("grp")
    tile = lax.axis_index("tile")

    def at_tile(by):
        return {"tile": lax.rem(tile + (by + n_tile), n_tile)}

    def at_grp(g):
        return {"grp": g}

    barrier = pltpu.get_barrier_semaphore()
    for by in EDGE_SHIFTS:
        pl.semaphore_signal(barrier, inc=1, device_id=at_tile(by), device_id_type=pl.DeviceIdType.MESH)
    for step in range(1, n_grp):
        pl.semaphore_signal(
            barrier, inc=1, device_id=at_grp(lax.rem(grp + step, n_grp)),
            device_id_type=pl.DeviceIdType.MESH,
        )
    pairs = ((dep_hbm, dep_ref), (frac_hbm, frac_ref), (x_hbm, x_ref), (lm_hbm, lm_ref), (cm_hbm, cm_ref))
    loads = [pltpu.make_async_copy(src, dst, load_sem.at[n]) for n, (src, dst) in enumerate(pairs)]
    for load in loads:
        load.start()
    for load in loads[:2]:
        load.wait()
    departure = dep_ref[...]
    target = (departure >> (cols.bit_length() - 1)) & (n_tile - 1)
    offset = ((target - tile + REACH) & (n_tile - 1)) - REACH
    values = [(departure & (cols - 1)).astype(F32)] + cubic_weights(frac_ref[...]) + [offset.astype(F32)]
    meta_ref[...] = jnp.zeros_like(meta_ref)
    for n, value in enumerate(values):
        for t in range(2):
            meta_ref[t, n : n + 1, :] = value[t : t + 1]

    sent = []
    metas = ([], [])

    def send(src, dst, ss, rs, where):
        copy = pltpu.make_async_remote_copy(
            src_ref=src, dst_ref=dst, send_sem=ss, recv_sem=rs,
            device_id=where, device_id_type=pl.DeviceIdType.MESH,
        )
        copy.start()
        sent.append(copy)
        return copy

    row8 = lax.broadcasted_iota(jnp.int32, (8, cols), 0)
    wanted = jnp.full((8, cols), -100.0, F32)
    for j, by in enumerate(SHIFTS):
        wanted = jnp.where(row8 == j, float(by), wanted)
    hot = jnp.concatenate(
        [jnp.where(wanted == meta_ref[1 - t, 5:6, :], 1.0, 0.0) for t in range(2)], axis=0
    )
    lane = 128
    r = lax.broadcasted_iota(jnp.int32, (lane, 2 * lane), 0)
    c = lax.broadcasted_iota(jnp.int32, (lane, 2 * lane), 1)
    counter = jnp.where((r < c) | (c >= lane), 1.0, 0.0).astype(BF16)
    stacked = jnp.concatenate([hot[:, i * lane : (i + 1) * lane] for i in range(cols // lane)], axis=0)
    counts = dot(stacked.astype(BF16), counter)
    total = jnp.zeros((16, lane), F32)
    for i in range(cols // lane):
        own = counts[16 * i : 16 * i + 16]
        before = own[:, :lane] + total
        total = total + own[:, lane:]
        mine = hot[:, i * lane : (i + 1) * lane] > 0.5
        slots[:, i * lane : (i + 1) * lane] = jnp.where(mine, before, -1.0).astype(jnp.int32)

    block = 128

    def build_pick(t, j):
        @pl.loop(0, half // block)
        def _(i):
            r = lax.broadcasted_iota(jnp.int32, (block, cols), 0) + i * block
            hit = r == slots[8 * t + j : 8 * t + j + 1, :]
            pick[t, j, pl.ds(pl.multiple_of(i * block, block), block), :] = jnp.where(hit, 1.0, 0.0).astype(BF16)

    def do_meta(t, j):
        whole = meta_ref[1 - t]
        a = whole.astype(BF16)
        rest = whole - a.astype(F32)
        parts = jnp.concatenate([a.astype(F32), rest], axis=0).astype(BF16)
        got = dot_nt(parts, pick[t, j])
        packed = got[:8] + got[8:]
        if j == REMOTE:
            meta_in[t, j] = packed
        else:
            meta_out[t, j] = packed
            metas[t].append(
                send(meta_out.at[t, j], meta_in.at[t, j], meta_ss.at[t, j], meta_rs.at[t, j], at_tile(SHIFTS[j]))
            )

    def build_spread(t, j):
        if j < REMOTE:
            metas[t][j].wait_recv()
        size = 128

        @pl.loop(0, cols // size)
        def _(i):
            cells = lax.broadcasted_iota(jnp.int32, (size, half), 0) + i * size
            place = meta_in[t, j, 0:1, :].astype(jnp.int32)
            value = jnp.zeros((size, half), F32)
            for k in range(4):
                value = jnp.where(cells == place + (k - 1), meta_in[t, j, 1 + k : 2 + k, :], value)
            high, low = split(value)
            at = pl.ds(pl.multiple_of(i * size, size), size)
            s_high[j, at, :] = high
            s_low[j, at, :] = low

    part_lev = lev // 2

    def swap(x):
        return pltpu.roll(x, part_lev, 1)

    def left(shape):
        return lax.broadcasted_iota(jnp.int32, shape, 1) < part_lev

    def twice(x, q):
        own = x[:, q * part_lev : (q + 1) * part_lev]
        return jnp.concatenate([own, own], axis=1)

    def deposit(t, q, j, first):
        both = rows_in[t, q, j]
        high = both.astype(BF16).astype(F32)
        low = both - high
        on_left = left(both.shape)
        rows_hl[: half // 2, :] = jnp.where(on_left, high, swap(low)).astype(BF16)
        rows_hl[half // 2 :, :] = jnp.where(on_left, swap(high), low).astype(BF16)
        size = 512

        @pl.loop(0, cols // size)
        def _(i):
            at = pl.ds(pl.multiple_of(i * size, size), size)
            part = dot(s_high[j, at, :], rows_hl[...]) + dot(s_low[j, at, :], rows_hl[...])
            if first:
                land[q, at, :] = part
            else:
                land[q, at, :] += part

    def close(t, q, edges):
        land[q] = land[q] + swap(land[q])
        sums = edge[t, len(edges)]
        for n, copy in enumerate(edges):
            if q == 0:
                copy.wait_recv()
            sums = sums + edge_in[t, n]
        sums = twice(sums, q)
        r = lax.broadcasted_iota(jnp.int32, (8, lev), 0)
        land[q, 0:8, :] += jnp.where(r < 2, sums, 0.0)
        land[q, cols - 8 : cols, :] += jnp.where(r == 7, sums[2:3], 0.0)

    def send_edges(t):
        place = meta_ref[1 - t, 0:1, :]
        w = [meta_ref[1 - t, 1 + k : 2 + k, :] for k in range(4)]
        offset = meta_ref[1 - t, 5:6, :]
        last = place == float(cols - 1)
        forward = jnp.where(last, w[2], jnp.where(place == float(cols - 2), w[3], 0.0))
        forward2 = jnp.where(last, w[3], 0.0)
        backward = jnp.where(place == 0.0, w[0], 0.0)
        blocks = []
        for by in EDGE_SHIFTS + (0, 0):
            near = offset == float(by - 1)
            value = jnp.where(row8 == 0, jnp.where(near, forward, 0.0), 0.0)
            value = jnp.where(row8 == 1, jnp.where(near, forward2, 0.0), value)
            value = jnp.where(row8 == 2, jnp.where(offset == float(by + 1), backward, 0.0), value)
            blocks.append(value)
        high, low = split(jnp.concatenate(blocks, axis=0))
        wide = dot(high, lifted[...])
        sums = wide[:, :lev] + wide[:, lev:] + dot(low, lifted[:, :lev])
        copies = []
        for n, by in enumerate(EDGE_SHIFTS):
            edge[t, n] = sums[8 * n : 8 * n + 8]
            copies.append(send(edge.at[t, n], edge_in.at[t, n], edge_ss.at[t, n], edge_rs.at[t, n], at_tile(by)))
        n = len(EDGE_SHIFTS)
        edge[t, n] = sums[8 * n : 8 * n + 8]
        return copies

    def transport(t, whole, exchange_first, exchange_last):
        m_high, m_low = split(lm_ref[1 - t])
        f_high, f_low = split(whole)
        lift = dot_nt(f_high, m_high) + dot_nt(f_low, m_high) + dot_nt(f_high, m_low)
        l_high, l_low = split(lift)
        lifted[:, :lev] = l_high
        lifted[:, lev:] = l_low
        on_left = left((half // 2, lev))
        copies = ([], [])

        def send_rows(q, j):
            copies[q].append(
                send(
                    rows_out.at[t, q, j], rows_in.at[t, q, j], rows_ss.at[t, q, j], rows_rs.at[t, q, j],
                    at_tile(SHIFTS[j]),
                )
            )

        for j in range(REMOTE + 1):
            if t == 0:
                build_pick(t, j)
                if j == 0:
                    pl.semaphore_wait(barrier, len(EDGE_SHIFTS) + n_grp - 1)
                do_meta(t, j)
            both = dot(pick[t, j], lifted[...])
            packed = both[:, :lev] + both[:, lev:]
            top, bottom = packed[: half // 2], packed[half // 2 :]
            into = rows_out if j < REMOTE else rows_in
            into[t, 0, j] = jnp.where(on_left, top, swap(bottom))
            into[t, 1, j] = jnp.where(on_left, swap(top), bottom)
            if j < REMOTE:
                send_rows(0, j)
        edges = send_edges(t)
        for j in range(REMOTE):
            send_rows(1, j)
        if t == 0:
            build_spread(t, REMOTE)
        for q in range(2):
            deposit(t, q, REMOTE, True)
        if t == 0:
            for j in range(REMOTE):
                build_spread(t, j)
        for q in range(2):
            for j in ARRIVE:
                copies[q][j].wait_recv()
                deposit(t, q, j, False)
            close(t, q, edges)
            (exchange_first, exchange_last)[q]()

    def coarse(b, e, q):
        return twice(cm_ref[b, pl.ds(e, 1), :], q)

    flip_x = grp + 1 - 2 * lax.rem(grp, 2)
    flip_y = lax.rem(grp + 2, n_grp)
    chunks = []
    for n in range(CHUNKS):
        near, far = ((flip_x, flip_y), (flip_y, flip_x))[n % 2]
        chunks.append((n, pl.ds(n * (half // CHUNKS), half // CHUNKS), near, far))
    firsts = ([], [])
    lasts = ([], [])

    def pack_part(q):
        grp_out[q] = jnp.where(left((half, lev)), land[q, :half, :], land[q, half:, :])

    def start(q):
        pack_part(q)
        for n, at, near, far in chunks:
            firsts[q].append(
                send(grp_out.at[q, at], grp_in.at[q, 0, at], grp_ss.at[q, 0, n], grp_rs.at[q, 0, n], at_grp(near))
            )

    def pass_on(q):
        for n, at, near, far in chunks:
            firsts[q][n].wait_recv()
            grp_mid[q, at, :] = coarse(far, grp, q) * grp_out[q, at, :] + coarse(far, near, q) * grp_in[q, 0, at, :]
            lasts[q].append(
                send(grp_mid.at[q, at], grp_last.at[q, at], grp_ss.at[q, 1, n], grp_rs.at[q, 1, n], at_grp(far))
            )
        for n, at, near, far in chunks:
            field[q, at, :] = coarse(grp, grp, q) * grp_out[q, at, :] + coarse(grp, near, q) * grp_in[q, 0, at, :]

    def finish(q):
        for n, at, near, far in chunks:
            lasts[q][n].wait_recv()
            field[q, at, :] += grp_last[q, at, :]

    def start_any(q):
        pack_part(q)
        for step in range(1, n_grp):
            to = lax.rem(grp + step, n_grp)
            firsts[q].append(
                send(grp_out.at[q], grp_in.at[q, step - 1], grp_ss.at[q, step - 1, 0], grp_rs.at[q, step - 1, 0], at_grp(to))
            )

    def finish_any(q):
        field[q] = coarse(grp, grp, q) * grp_out[q]
        for step in range(1, n_grp):
            firsts[q][step - 1].wait_recv()
            field[q] += coarse(grp, lax.rem(grp + n_grp - step, n_grp), q) * grp_in[q, step - 1]

    square = n_grp == 4

    def exchange_first():
        (start if square else start_any)(0)
        for j in range(REMOTE + 1):
            build_pick(1, j)
        if square:
            pass_on(0)

    def exchange_last():
        (start if square else start_any)(1)
        for j in range(REMOTE + 1):
            do_meta(1, j)
        if square:
            pass_on(1)
        for j in range(REMOTE + 1):
            build_spread(1, j)
        for q in range(2):
            (finish if square else finish_any)(q)

    def nothing():
        pass

    for load in loads[2:]:
        load.wait()
    transport(0, x_ref[...], exchange_first, exchange_last)
    on_left = left((half, lev))
    whole = jnp.concatenate(
        [jnp.where(on_left, field[0], swap(field[1])), jnp.where(on_left, swap(field[0]), field[1])], axis=0
    )
    transport(1, whole, nothing, nothing)
    out_ref[...] = jnp.where(left((cols, lev)), land[0], land[1])
    for copy in sent:
        copy.wait_send()


def body(n_grp, n_tile, adjoint_in, departure, fraction, level_map, coarse_map):
    cols, lev = adjoint_in.shape
    half = cols // 2
    n_in = 1 if n_grp == 4 else n_grp - 1
    dma = pltpu.SemaphoreType.DMA
    return pl.pallas_call(
        functools.partial(kernel, n_grp, n_tile),
        out_shape=jax.ShapeDtypeStruct((cols, lev), F32),
        in_specs=[pl.BlockSpec(memory_space=pltpu.HBM)] * 5,
        out_specs=pl.BlockSpec(memory_space=pltpu.VMEM),
        scratch_shapes=[
            pltpu.VMEM((cols, lev), F32),
            pltpu.VMEM((2, cols), jnp.int32),
            pltpu.VMEM((2, cols), F32),
            pltpu.VMEM(level_map.shape, F32),
            pltpu.VMEM((n_grp, n_grp, lev), F32),
            pltpu.VMEM((2, 8, cols), F32),
            pltpu.VMEM((16, cols), jnp.int32),
            pltpu.VMEM((2, REMOTE + 1, half, cols), BF16),
            pltpu.VMEM((cols, 2 * lev), BF16),
            pltpu.VMEM((2, 2, REMOTE, half // 2, lev), F32),
            pltpu.VMEM((2, 2, REMOTE + 1, half // 2, lev), F32),
            pltpu.VMEM((2, REMOTE, 8, half), F32),
            pltpu.VMEM((2, REMOTE + 1, 8, half), F32),
            pltpu.VMEM((half, lev), BF16),
            pltpu.VMEM((REMOTE + 1, cols, half), BF16),
            pltpu.VMEM((REMOTE + 1, cols, half), BF16),
            pltpu.VMEM((2, cols, lev), F32),
            pltpu.VMEM((2, len(EDGE_SHIFTS) + 1, 8, lev), F32),
            pltpu.VMEM((2, len(EDGE_SHIFTS), 8, lev), F32),
            pltpu.VMEM((2, half, lev), F32),
            pltpu.VMEM((2, half, lev), F32),
            pltpu.VMEM((2, n_in, half, lev), F32),
            pltpu.VMEM((2, half, lev), F32),
            pltpu.VMEM((2, half, lev), F32),
            dma((5,)),
            dma((2, 2, REMOTE)),
            dma((2, 2, REMOTE)),
            dma((2, REMOTE)),
            dma((2, REMOTE)),
            dma((2, len(EDGE_SHIFTS))),
            dma((2, len(EDGE_SHIFTS))),
            dma((2, max(2, n_grp - 1), CHUNKS)),
            dma((2, max(2, n_grp - 1), CHUNKS)),
        ],
        compiler_params=pltpu.CompilerParams(
            collective_id=0, has_side_effects=True, vmem_limit_bytes=48 * 2 ** 20
        ),
    )(adjoint_in, departure, fraction, level_map, coarse_map.transpose(1, 2, 0))


def solution(mesh):
    return jax.shard_map(
        functools.partial(body, mesh.shape["grp"], mesh.shape["tile"]),
        mesh=mesh,
        in_specs=(
            P(("grp", "tile"), None),
            P(None, ("grp", "tile")),
            P(None, ("grp", "tile")),
            P(),
            P(),
        ),
        out_specs=P(("grp", "tile"), None),
        check_vma=False,
    )
```

```python
import functools

import jax
import jax.numpy as jnp
from jax import lax
from jax.experimental import pallas as pl
from jax.experimental.pallas import tpu as pltpu
from jax.sharding import PartitionSpec as P

REACH = 2
SHIFTS = (2, -2, 1, -1, 0)
REMOTE = 4
EDGE_SHIFTS = (1, -1, 2, -2, 3, -3)
CHUNKS = 4
ARRIVE = (2, 3, 0, 1)
BF16 = jnp.bfloat16
F32 = jnp.float32


def cubic_weights(a):
    return [
        -a * (1.0 - a) * (2.0 - a) / 6.0,
        (1.0 + a) * (1.0 - a) * (2.0 - a) / 2.0,
        (1.0 + a) * a * (2.0 - a) / 2.0,
        -(1.0 + a) * a * (1.0 - a) / 6.0,
    ]


def split(x):
    high = x.astype(BF16)
    return high, (x - high.astype(F32)).astype(BF16)


def dot(a, b):
    return jnp.dot(a, b, preferred_element_type=F32)


def dot_nt(a, b):
    return lax.dot_general(a, b, (((1,), (1,)), ((), ())), preferred_element_type=F32)


def kernel(
    n_grp, n_tile, x_hbm, dep_hbm, frac_hbm, lm_hbm, cm_hbm, out_ref,
    x_ref, dep_ref, frac_ref, lm_ref, cm_ref, meta_ref,
    slots, pick, lifted, rows_out, rows_in, meta_out, meta_in, rows_hl,
    s_high, s_low, land, edge, edge_in, field, grp_out, grp_in, grp_mid, grp_last,
    load_sem, rows_ss, rows_rs, meta_ss, meta_rs, edge_ss, edge_rs, grp_ss, grp_rs,
):
    cols, lev = x_ref.shape
    half = cols // 2
    grp = lax.axis_index("grp")
    tile = lax.axis_index("tile")

    def at_tile(by):
        return {"tile": lax.rem(tile + (by + n_tile), n_tile)}

    def at_grp(g):
        return {"grp": g}

    barrier = pltpu.get_barrier_semaphore()
    for by in EDGE_SHIFTS:
        pl.semaphore_signal(barrier, inc=1, device_id=at_tile(by), device_id_type=pl.DeviceIdType.MESH)
    for step in range(1, n_grp):
        pl.semaphore_signal(
            barrier, inc=1, device_id=at_grp(lax.rem(grp + step, n_grp)),
            device_id_type=pl.DeviceIdType.MESH,
        )
    pairs = ((dep_hbm, dep_ref), (frac_hbm, frac_ref), (x_hbm, x_ref), (lm_hbm, lm_ref), (cm_hbm, cm_ref))
    loads = [pltpu.make_async_copy(src, dst, load_sem.at[n]) for n, (src, dst) in enumerate(pairs)]
    for load in loads:
        load.start()
    for load in loads[:2]:
        load.wait()
    departure = dep_ref[...]
    target = (departure >> (cols.bit_length() - 1)) & (n_tile - 1)
    offset = ((target - tile + REACH) & (n_tile - 1)) - REACH
    values = [(departure & (cols - 1)).astype(F32)] + cubic_weights(frac_ref[...]) + [offset.astype(F32)]
    meta_ref[...] = jnp.zeros_like(meta_ref)
    for n, value in enumerate(values):
        for t in range(2):
            meta_ref[t, n : n + 1, :] = value[t : t + 1]

    sent = []
    left_already = []
    metas = ([], [])

    def send(src, dst, ss, rs, where):
        copy = pltpu.make_async_remote_copy(
            src_ref=src, dst_ref=dst, send_sem=ss, recv_sem=rs,
            device_id=where, device_id_type=pl.DeviceIdType.MESH,
        )
        copy.start()
        sent.append(copy)
        return copy

    row8 = lax.broadcasted_iota(jnp.int32, (8, cols), 0)
    wanted = jnp.full((8, cols), -100.0, F32)
    for j, by in enumerate(SHIFTS):
        wanted = jnp.where(row8 == j, float(by), wanted)
    hot = jnp.concatenate(
        [jnp.where(wanted == meta_ref[1 - t, 5:6, :], 1.0, 0.0) for t in range(2)], axis=0
    )
    lane = 128
    r = lax.broadcasted_iota(jnp.int32, (lane, 2 * lane), 0)
    c = lax.broadcasted_iota(jnp.int32, (lane, 2 * lane), 1)
    counter = jnp.where((r < c) | (c >= lane), 1.0, 0.0).astype(BF16)
    stacked = jnp.concatenate([hot[:, i * lane : (i + 1) * lane] for i in range(cols // lane)], axis=0)
    counts = dot(stacked.astype(BF16), counter)
    total = jnp.zeros((16, lane), F32)
    for i in range(cols // lane):
        own = counts[16 * i : 16 * i + 16]
        before = own[:, :lane] + total
        total = total + own[:, lane:]
        mine = hot[:, i * lane : (i + 1) * lane] > 0.5
        slots[:, i * lane : (i + 1) * lane] = jnp.where(mine, before, -1.0).astype(jnp.int32)

    block = 128

    def build_pick(t, j):
        @pl.loop(0, half // block)
        def _(i):
            r = lax.broadcasted_iota(jnp.int32, (block, cols), 0) + i * block
            hit = r == slots[8 * t + j : 8 * t + j + 1, :]
            pick[t, j, pl.ds(pl.multiple_of(i * block, block), block), :] = jnp.where(hit, 1.0, 0.0).astype(BF16)

    def do_meta(t, j):
        whole = meta_ref[1 - t]
        a = whole.astype(BF16)
        rest = whole - a.astype(F32)
        parts = jnp.concatenate([a.astype(F32), rest], axis=0).astype(BF16)
        got = dot_nt(parts, pick[t, j])
        packed = got[:8] + got[8:]
        if j == REMOTE:
            meta_in[t, j] = packed
        else:
            meta_out[t, j] = packed
            metas[t].append(
                send(meta_out.at[t, j], meta_in.at[t, j], meta_ss.at[t, j], meta_rs.at[t, j], at_tile(SHIFTS[j]))
            )

    def build_spread(t, j):
        if j < REMOTE:
            metas[t][j].wait_recv()
        size = 128

        @pl.loop(0, cols // size)
        def _(i):
            cells = lax.broadcasted_iota(jnp.int32, (size, half), 0) + i * size
            place = meta_in[t, j, 0:1, :].astype(jnp.int32)
            value = jnp.zeros((size, half), F32)
            for k in range(4):
                value = jnp.where(cells == place + (k - 1), meta_in[t, j, 1 + k : 2 + k, :], value)
            high, low = split(value)
            at = pl.ds(pl.multiple_of(i * size, size), size)
            s_high[j, at, :] = high
            s_low[j, at, :] = low

    part_lev = lev // 2

    def swap(x):
        return pltpu.roll(x, part_lev, 1)

    def left(shape):
        return lax.broadcasted_iota(jnp.int32, shape, 1) < part_lev

    def twice(x, q):
        own = x[:, q * part_lev : (q + 1) * part_lev]
        return jnp.concatenate([own, own], axis=1)

    def deposit(t, q, j, first):
        both = rows_in[t, q, j]
        high = both.astype(BF16).astype(F32)
        low = both - high
        on_left = left(both.shape)
        rows_hl[: half // 2, :] = jnp.where(on_left, high, swap(low)).astype(BF16)
        rows_hl[half // 2 :, :] = jnp.where(on_left, swap(high), low).astype(BF16)
        size = 512

        @pl.loop(0, cols // size)
        def _(i):
            at = pl.ds(pl.multiple_of(i * size, size), size)
            part = dot(s_high[j, at, :], rows_hl[...]) + dot(s_low[j, at, :], rows_hl[...])
            if first:
                land[q, at, :] = part
            else:
                land[q, at, :] += part

    def close(t, q, edges):
        land[q] = land[q] + swap(land[q])
        sums = edge[t, len(edges)]
        for n, copy in enumerate(edges):
            if q == 0:
                copy.wait_recv()
            sums = sums + edge_in[t, n]
        sums = twice(sums, q)
        r = lax.broadcasted_iota(jnp.int32, (8, lev), 0)
        land[q, 0:8, :] += jnp.where(r < 2, sums, 0.0)
        land[q, cols - 8 : cols, :] += jnp.where(r == 7, sums[2:3], 0.0)

    def send_edges(t):
        place = meta_ref[1 - t, 0:1, :]
        w = [meta_ref[1 - t, 1 + k : 2 + k, :] for k in range(4)]
        offset = meta_ref[1 - t, 5:6, :]
        last = place == float(cols - 1)
        forward = jnp.where(last, w[2], jnp.where(place == float(cols - 2), w[3], 0.0))
        forward2 = jnp.where(last, w[3], 0.0)
        backward = jnp.where(place == 0.0, w[0], 0.0)
        blocks = []
        for by in EDGE_SHIFTS + (0, 0):
            near = offset == float(by - 1)
            value = jnp.where(row8 == 0, jnp.where(near, forward, 0.0), 0.0)
            value = jnp.where(row8 == 1, jnp.where(near, forward2, 0.0), value)
            value = jnp.where(row8 == 2, jnp.where(offset == float(by + 1), backward, 0.0), value)
            blocks.append(value)
        high, low = split(jnp.concatenate(blocks, axis=0))
        wide = dot(high, lifted[...])
        sums = wide[:, :lev] + wide[:, lev:] + dot(low, lifted[:, :lev])
        copies = []
        for n, by in enumerate(EDGE_SHIFTS):
            edge[t, n] = sums[8 * n : 8 * n + 8]
            copies.append(send(edge.at[t, n], edge_in.at[t, n], edge_ss.at[t, n], edge_rs.at[t, n], at_tile(by)))
        n = len(EDGE_SHIFTS)
        edge[t, n] = sums[8 * n : 8 * n + 8]
        return copies

    def transport(t, whole, exchange_first, exchange_last):
        m_high, m_low = split(lm_ref[1 - t])
        f_high, f_low = split(whole)
        lift = dot_nt(f_high, m_high) + dot_nt(f_low, m_high) + dot_nt(f_high, m_low)
        l_high, l_low = split(lift)
        lifted[:, :lev] = l_high
        lifted[:, lev:] = l_low
        on_left = left((half // 2, lev))
        copies = ({}, {})

        def send_rows(q, j):
            copies[q][j] = (
                send(
                    rows_out.at[t, q, j], rows_in.at[t, q, j], rows_ss.at[t, q, j], rows_rs.at[t, q, j],
                    at_tile(SHIFTS[j]),
                )
            )

        for j in range(REMOTE + 1):
            if t == 0:
                build_pick(t, j)
                if j == 0:
                    pl.semaphore_wait(barrier, len(EDGE_SHIFTS) + n_grp - 1)
            both = dot(pick[t, j], lifted[...])
            packed = both[:, :lev] + both[:, lev:]
            top, bottom = packed[: half // 2], packed[half // 2 :]
            into = rows_out if j < REMOTE else rows_in
            into[t, 0, j] = jnp.where(on_left, top, swap(bottom))
            into[t, 1, j] = jnp.where(on_left, swap(top), bottom)
            if j < REMOTE:
                send_rows(0, j)
        if t == 0:
            for j in range(REMOTE + 1):
                do_meta(t, j)
        edges = send_edges(t)
        if t == 0:
            build_spread(t, REMOTE)
        for q in range(2):
            deposit(t, q, REMOTE, True)
        if t == 0:
            for j in range(REMOTE):
                build_spread(t, j)
        for j in (2, 3, 0, 1):
            copies[0][j].wait_send()
            left_already.append(id(copies[0][j]))
            send_rows(1, j)
        for q in range(2):
            for j in ARRIVE:
                copies[q][j].wait_recv()
                deposit(t, q, j, False)
            close(t, q, edges)
            (exchange_first, exchange_last)[q]()

    def coarse(b, e, q):
        return twice(cm_ref[b, pl.ds(e, 1), :], q)

    flip_x = grp + 1 - 2 * lax.rem(grp, 2)
    flip_y = lax.rem(grp + 2, n_grp)
    chunks = []
    for n in range(CHUNKS):
        near, far = ((flip_x, flip_y), (flip_y, flip_x))[n % 2]
        chunks.append((n, pl.ds(n * (half // CHUNKS), half // CHUNKS), near, far))
    firsts = ([], [])
    lasts = ([], [])

    def pack_part(q):
        grp_out[q] = jnp.where(left((half, lev)), land[q, :half, :], land[q, half:, :])

    def start(q):
        pack_part(q)
        for n, at, near, far in chunks:
            firsts[q].append(
                send(grp_out.at[q, at], grp_in.at[q, 0, at], grp_ss.at[q, 0, n], grp_rs.at[q, 0, n], at_grp(near))
            )

    def pass_on(q):
        for n, at, near, far in chunks:
            firsts[q][n].wait_recv()
            grp_mid[q, at, :] = coarse(far, grp, q) * grp_out[q, at, :] + coarse(far, near, q) * grp_in[q, 0, at, :]
            lasts[q].append(
                send(grp_mid.at[q, at], grp_last.at[q, at], grp_ss.at[q, 1, n], grp_rs.at[q, 1, n], at_grp(far))
            )
        for n, at, near, far in chunks:
            field[q, at, :] = coarse(grp, grp, q) * grp_out[q, at, :] + coarse(grp, near, q) * grp_in[q, 0, at, :]

    def finish(q):
        for n, at, near, far in chunks:
            lasts[q][n].wait_recv()
            field[q, at, :] += grp_last[q, at, :]

    def start_any(q):
        pack_part(q)
        for step in range(1, n_grp):
            to = lax.rem(grp + step, n_grp)
            firsts[q].append(
                send(grp_out.at[q], grp_in.at[q, step - 1], grp_ss.at[q, step - 1, 0], grp_rs.at[q, step - 1, 0], at_grp(to))
            )

    def finish_any(q):
        field[q] = coarse(grp, grp, q) * grp_out[q]
        for step in range(1, n_grp):
            firsts[q][step - 1].wait_recv()
            field[q] += coarse(grp, lax.rem(grp + n_grp - step, n_grp), q) * grp_in[q, step - 1]

    square = n_grp == 4

    def exchange_first():
        (start if square else start_any)(0)
        for j in range(REMOTE + 1):
            build_pick(1, j)
        if square:
            pass_on(0)
        for j in range(REMOTE + 1):
            do_meta(1, j)

    def exchange_last():
        (start if square else start_any)(1)
        for j in (REMOTE, 0):
            build_spread(1, j)
        if square:
            pass_on(1)
        for j in range(1, REMOTE):
            build_spread(1, j)
        for q in range(2):
            (finish if square else finish_any)(q)

    def nothing():
        pass

    for load in loads[2:]:
        load.wait()
    transport(0, x_ref[...], exchange_first, exchange_last)
    on_left = left((half, lev))
    whole = jnp.concatenate(
        [jnp.where(on_left, field[0], swap(field[1])), jnp.where(on_left, swap(field[0]), field[1])], axis=0
    )
    transport(1, whole, nothing, nothing)
    out_ref[...] = jnp.where(left((cols, lev)), land[0], land[1])
    for copy in sent:
        if id(copy) not in left_already:
            copy.wait_send()


def body(n_grp, n_tile, adjoint_in, departure, fraction, level_map, coarse_map):
    cols, lev = adjoint_in.shape
    half = cols // 2
    n_in = 1 if n_grp == 4 else n_grp - 1
    dma = pltpu.SemaphoreType.DMA
    return pl.pallas_call(
        functools.partial(kernel, n_grp, n_tile),
        out_shape=jax.ShapeDtypeStruct((cols, lev), F32),
        in_specs=[pl.BlockSpec(memory_space=pltpu.HBM)] * 5,
        out_specs=pl.BlockSpec(memory_space=pltpu.VMEM),
        scratch_shapes=[
            pltpu.VMEM((cols, lev), F32),
            pltpu.VMEM((2, cols), jnp.int32),
            pltpu.VMEM((2, cols), F32),
            pltpu.VMEM(level_map.shape, F32),
            pltpu.VMEM((n_grp, n_grp, lev), F32),
            pltpu.VMEM((2, 8, cols), F32),
            pltpu.VMEM((16, cols), jnp.int32),
            pltpu.VMEM((2, REMOTE + 1, half, cols), BF16),
            pltpu.VMEM((cols, 2 * lev), BF16),
            pltpu.VMEM((2, 2, REMOTE, half // 2, lev), F32),
            pltpu.VMEM((2, 2, REMOTE + 1, half // 2, lev), F32),
            pltpu.VMEM((2, REMOTE, 8, half), F32),
            pltpu.VMEM((2, REMOTE + 1, 8, half), F32),
            pltpu.VMEM((half, lev), BF16),
            pltpu.VMEM((REMOTE + 1, cols, half), BF16),
            pltpu.VMEM((REMOTE + 1, cols, half), BF16),
            pltpu.VMEM((2, cols, lev), F32),
            pltpu.VMEM((2, len(EDGE_SHIFTS) + 1, 8, lev), F32),
            pltpu.VMEM((2, len(EDGE_SHIFTS), 8, lev), F32),
            pltpu.VMEM((2, half, lev), F32),
            pltpu.VMEM((2, half, lev), F32),
            pltpu.VMEM((2, n_in, half, lev), F32),
            pltpu.VMEM((2, half, lev), F32),
            pltpu.VMEM((2, half, lev), F32),
            dma((5,)),
            dma((2, 2, REMOTE)),
            dma((2, 2, REMOTE)),
            dma((2, REMOTE)),
            dma((2, REMOTE)),
            dma((2, len(EDGE_SHIFTS))),
            dma((2, len(EDGE_SHIFTS))),
            dma((2, max(2, n_grp - 1), CHUNKS)),
            dma((2, max(2, n_grp - 1), CHUNKS)),
        ],
        compiler_params=pltpu.CompilerParams(
            collective_id=0, has_side_effects=True, vmem_limit_bytes=60 * 2 ** 20
        ),
    )(adjoint_in, departure, fraction, level_map, coarse_map.transpose(1, 2, 0))


def solution(mesh):
    return jax.shard_map(
        functools.partial(body, mesh.shape["grp"], mesh.shape["tile"]),
        mesh=mesh,
        in_specs=(
            P(("grp", "tile"), None),
            P(None, ("grp", "tile")),
            P(None, ("grp", "tile")),
            P(),
            P(),
        ),
        out_specs=P(("grp", "tile"), None),
        check_vma=False,
    )
```

```python
import functools

import jax
import jax.numpy as jnp
from jax import lax
from jax.experimental import pallas as pl
from jax.experimental.pallas import tpu as pltpu
from jax.sharding import PartitionSpec as P

REACH = 2
SHIFTS = (2, -2, 1, -1, 0)
REMOTE = 4
EDGE_SHIFTS = (1, -1, 2, -2, 3, -3)
CHUNKS = 4
ARRIVE = (2, 3, 0, 1)
BF16 = jnp.bfloat16
F32 = jnp.float32


def cubic_weights(a):
    return [
        -a * (1.0 - a) * (2.0 - a) / 6.0,
        (1.0 + a) * (1.0 - a) * (2.0 - a) / 2.0,
        (1.0 + a) * a * (2.0 - a) / 2.0,
        -(1.0 + a) * a * (1.0 - a) / 6.0,
    ]


def split(x):
    high = x.astype(BF16)
    return high, (x - high.astype(F32)).astype(BF16)


def dot(a, b):
    return jnp.dot(a, b, preferred_element_type=F32)


def dot_nt(a, b):
    return lax.dot_general(a, b, (((1,), (1,)), ((), ())), preferred_element_type=F32)


def kernel(
    n_grp, n_tile, x_hbm, dep_hbm, frac_hbm, lm_hbm, cm_hbm, out_ref,
    x_ref, dep_ref, frac_ref, lm_ref, cm_ref, meta_ref,
    slots, pick, meta_cols, lifted, rows_out, rows_in, meta_out, meta_in, rows_hl,
    s_high, s_low, land, edge, edge_in, field, grp_out, grp_in, grp_mid, grp_last,
    load_sem, rows_ss, rows_rs, meta_ss, meta_rs, edge_ss, edge_rs, grp_ss, grp_rs,
):
    cols, lev = x_ref.shape
    half = cols // 2
    grp = lax.axis_index("grp")
    tile = lax.axis_index("tile")

    def at_tile(by):
        return {"tile": lax.rem(tile + (by + n_tile), n_tile)}

    def at_grp(g):
        return {"grp": g}

    barrier = pltpu.get_barrier_semaphore()
    for by in EDGE_SHIFTS:
        pl.semaphore_signal(barrier, inc=1, device_id=at_tile(by), device_id_type=pl.DeviceIdType.MESH)
    for step in range(1, n_grp):
        pl.semaphore_signal(
            barrier, inc=1, device_id=at_grp(lax.rem(grp + step, n_grp)),
            device_id_type=pl.DeviceIdType.MESH,
        )
    pairs = ((dep_hbm, dep_ref), (frac_hbm, frac_ref), (x_hbm, x_ref), (lm_hbm, lm_ref), (cm_hbm, cm_ref))
    loads = [pltpu.make_async_copy(src, dst, load_sem.at[n]) for n, (src, dst) in enumerate(pairs)]
    for load in loads:
        load.start()
    for load in loads[:2]:
        load.wait()
    departure = dep_ref[...]
    target = (departure >> (cols.bit_length() - 1)) & (n_tile - 1)
    offset = ((target - tile + REACH) & (n_tile - 1)) - REACH
    values = [(departure & (cols - 1)).astype(F32)] + cubic_weights(frac_ref[...]) + [offset.astype(F32)]
    meta_ref[...] = jnp.zeros_like(meta_ref)
    for n, value in enumerate(values):
        for t in range(2):
            meta_ref[t, n : n + 1, :] = value[t : t + 1]

    sent = []
    left_already = []
    metas = ([], [])

    def send(src, dst, ss, rs, where):
        copy = pltpu.make_async_remote_copy(
            src_ref=src, dst_ref=dst, send_sem=ss, recv_sem=rs,
            device_id=where, device_id_type=pl.DeviceIdType.MESH,
        )
        copy.start()
        sent.append(copy)
        return copy

    row8 = lax.broadcasted_iota(jnp.int32, (8, cols), 0)
    wanted = jnp.full((8, cols), -100.0, F32)
    for j, by in enumerate(SHIFTS):
        wanted = jnp.where(row8 == j, float(by), wanted)
    hot = jnp.concatenate(
        [jnp.where(wanted == meta_ref[1 - t, 5:6, :], 1.0, 0.0) for t in range(2)], axis=0
    )
    lane = 128
    r = lax.broadcasted_iota(jnp.int32, (lane, 2 * lane), 0)
    c = lax.broadcasted_iota(jnp.int32, (lane, 2 * lane), 1)
    counter = jnp.where((r < c) | (c >= lane), 1.0, 0.0).astype(BF16)
    stacked = jnp.concatenate([hot[:, i * lane : (i + 1) * lane] for i in range(cols // lane)], axis=0)
    counts = dot(stacked.astype(BF16), counter)
    total = jnp.zeros((16, lane), F32)
    for i in range(cols // lane):
        own = counts[16 * i : 16 * i + 16]
        before = own[:, :lane] + total
        total = total + own[:, lane:]
        mine = hot[:, i * lane : (i + 1) * lane] > 0.5
        slots[:, i * lane : (i + 1) * lane] = jnp.where(mine, before, -1.0).astype(jnp.int32)

    block = 128

    def build_pick(t, j):
        @pl.loop(0, half // block)
        def _(i):
            r = lax.broadcasted_iota(jnp.int32, (block, lane), 0) + i * block
            at = pl.ds(pl.multiple_of(i * block, block), block)
            for n in range(0, cols, lane):
                hit = r == slots[8 * t + j : 8 * t + j + 1, n : n + lane]
                pick[t, j, at, n : n + lane] = jnp.where(hit, 1.0, 0.0).astype(BF16)

    def meta_columns(t):
        whole = meta_ref[1 - t]
        a = whole.astype(BF16).astype(F32)
        parts = jnp.concatenate([a, whole - a, jnp.zeros((lane - 16, cols), F32)], axis=0)
        meta_cols[t] = parts.T.astype(BF16)

    def do_meta(t, j):
        if j == 0:
            meta_columns(t)
        got = dot(pick[t, j], meta_cols[t]).T
        packed = got[:8] + got[8:16]
        if j == REMOTE:
            meta_in[t, j] = packed
        else:
            meta_out[t, j] = packed
            metas[t].append(
                send(meta_out.at[t, j], meta_in.at[t, j], meta_ss.at[t, j], meta_rs.at[t, j], at_tile(SHIFTS[j]))
            )

    def build_spread(t, j):
        if j < REMOTE:
            metas[t][j].wait_recv()
        size = 128

        @pl.loop(0, cols // size)
        def _(i):
            cells = lax.broadcasted_iota(jnp.int32, (size, lane), 0) + i * size
            at = pl.ds(pl.multiple_of(i * size, size), size)
            for n in range(0, half, lane):
                place = meta_in[t, j, 0:1, n : n + lane].astype(jnp.int32)
                value = jnp.zeros((size, lane), F32)
                for k in range(4):
                    value = jnp.where(cells == place + (k - 1), meta_in[t, j, 1 + k : 2 + k, n : n + lane], value)
                high, low = split(value)
                s_high[j, at, n : n + lane] = high
                s_low[j, at, n : n + lane] = low

    part_lev = lev // 2

    def swap(x):
        return pltpu.roll(x, part_lev, 1)

    def left(shape):
        return lax.broadcasted_iota(jnp.int32, shape, 1) < part_lev

    def twice(x, q):
        own = x[:, q * part_lev : (q + 1) * part_lev]
        return jnp.concatenate([own, own], axis=1)

    def deposit(t, q, j, first):
        both = rows_in[t, q, j]
        high = both.astype(BF16).astype(F32)
        low = both - high
        on_left = left(both.shape)
        rows_hl[: half // 2, :] = jnp.where(on_left, high, swap(low)).astype(BF16)
        rows_hl[half // 2 :, :] = jnp.where(on_left, swap(high), low).astype(BF16)
        size = 512

        @pl.loop(0, cols // size)
        def _(i):
            at = pl.ds(pl.multiple_of(i * size, size), size)
            part = dot(s_high[j, at, :], rows_hl[...]) + dot(s_low[j, at, :], rows_hl[...])
            if first:
                land[q, at, :] = part
            else:
                land[q, at, :] += part

    def close(t, q, edges):
        land[q] = land[q] + swap(land[q])
        sums = edge[t, len(edges)]
        for n, copy in enumerate(edges):
            if q == 0:
                copy.wait_recv()
            sums = sums + edge_in[t, n]
        sums = twice(sums, q)
        r = lax.broadcasted_iota(jnp.int32, (8, lev), 0)
        land[q, 0:8, :] += jnp.where(r < 2, sums, 0.0)
        land[q, cols - 8 : cols, :] += jnp.where(r == 7, sums[2:3], 0.0)

    def send_edges(t):
        place = meta_ref[1 - t, 0:1, :]
        w = [meta_ref[1 - t, 1 + k : 2 + k, :] for k in range(4)]
        offset = meta_ref[1 - t, 5:6, :]
        last = place == float(cols - 1)
        forward = jnp.where(last, w[2], jnp.where(place == float(cols - 2), w[3], 0.0))
        forward2 = jnp.where(last, w[3], 0.0)
        backward = jnp.where(place == 0.0, w[0], 0.0)
        blocks = []
        for by in EDGE_SHIFTS + (0, 0):
            near = offset == float(by - 1)
            value = jnp.where(row8 == 0, jnp.where(near, forward, 0.0), 0.0)
            value = jnp.where(row8 == 1, jnp.where(near, forward2, 0.0), value)
            value = jnp.where(row8 == 2, jnp.where(offset == float(by + 1), backward, 0.0), value)
            blocks.append(value)
        high, low = split(jnp.concatenate(blocks, axis=0))
        wide = dot(high, lifted[...])
        sums = wide[:, :lev] + wide[:, lev:] + dot(low, lifted[:, :lev])
        copies = []
        for n, by in enumerate(EDGE_SHIFTS):
            edge[t, n] = sums[8 * n : 8 * n + 8]
            copies.append(send(edge.at[t, n], edge_in.at[t, n], edge_ss.at[t, n], edge_rs.at[t, n], at_tile(by)))
        n = len(EDGE_SHIFTS)
        edge[t, n] = sums[8 * n : 8 * n + 8]
        return copies

    def transport(t, whole, exchange_first, exchange_last):
        m_high, m_low = split(lm_ref[1 - t])
        f_high, f_low = split(whole)
        lift = dot_nt(f_high, m_high) + dot_nt(f_low, m_high) + dot_nt(f_high, m_low)
        l_high, l_low = split(lift)
        lifted[:, :lev] = l_high
        lifted[:, lev:] = l_low
        on_left = left((half // 2, lev))
        copies = ({}, {})

        def send_rows(q, j):
            copies[q][j] = (
                send(
                    rows_out.at[t, q, j], rows_in.at[t, q, j], rows_ss.at[t, q, j], rows_rs.at[t, q, j],
                    at_tile(SHIFTS[j]),
                )
            )

        for j in range(REMOTE + 1):
            if t == 0:
                build_pick(t, j)
                if j == 0:
                    pl.semaphore_wait(barrier, len(EDGE_SHIFTS) + n_grp - 1)
            both = dot(pick[t, j], lifted[...])
            packed = both[:, :lev] + both[:, lev:]
            top, bottom = packed[: half // 2], packed[half // 2 :]
            into = rows_out if j < REMOTE else rows_in
            into[t, 0, j] = jnp.where(on_left, top, swap(bottom))
            into[t, 1, j] = jnp.where(on_left, swap(top), bottom)
            if j < REMOTE:
                send_rows(0, j)
        if t == 0:
            for j in range(REMOTE + 1):
                do_meta(t, j)
        edges = send_edges(t)
        if t == 0:
            build_spread(t, REMOTE)
        for q in range(2):
            deposit(t, q, REMOTE, True)
        if t == 0:
            for j in range(REMOTE):
                build_spread(t, j)
        for j in (2, 3, 0, 1):
            copies[0][j].wait_send()
            left_already.append(id(copies[0][j]))
            send_rows(1, j)
        for q in range(2):
            for j in ARRIVE:
                copies[q][j].wait_recv()
                deposit(t, q, j, False)
            close(t, q, edges)
            (exchange_first, exchange_last)[q]()

    def coarse(b, e, q):
        return twice(cm_ref[b, pl.ds(e, 1), :], q)

    flip_x = grp + 1 - 2 * lax.rem(grp, 2)
    flip_y = lax.rem(grp + 2, n_grp)
    chunks = []
    for n in range(CHUNKS):
        near, far = ((flip_x, flip_y), (flip_y, flip_x))[n % 2]
        chunks.append((n, pl.ds(n * (half // CHUNKS), half // CHUNKS), near, far))
    firsts = ([], [])
    lasts = ([], [])

    def pack_part(q):
        grp_out[q] = jnp.where(left((half, lev)), land[q, :half, :], land[q, half:, :])

    def start(q):
        pack_part(q)
        for n, at, near, far in chunks:
            firsts[q].append(
                send(grp_out.at[q, at], grp_in.at[q, 0, at], grp_ss.at[q, 0, n], grp_rs.at[q, 0, n], at_grp(near))
            )

    def pass_on(q):
        for n, at, near, far in chunks:
            firsts[q][n].wait_recv()
            grp_mid[q, at, :] = coarse(far, grp, q) * grp_out[q, at, :] + coarse(far, near, q) * grp_in[q, 0, at, :]
            lasts[q].append(
                send(grp_mid.at[q, at], grp_last.at[q, at], grp_ss.at[q, 1, n], grp_rs.at[q, 1, n], at_grp(far))
            )
        for n, at, near, far in chunks:
            field[q, at, :] = coarse(grp, grp, q) * grp_out[q, at, :] + coarse(grp, near, q) * grp_in[q, 0, at, :]

    def finish(q):
        for n, at, near, far in chunks:
            lasts[q][n].wait_recv()
            field[q, at, :] += grp_last[q, at, :]

    def start_any(q):
        pack_part(q)
        for step in range(1, n_grp):
            to = lax.rem(grp + step, n_grp)
            firsts[q].append(
                send(grp_out.at[q], grp_in.at[q, step - 1], grp_ss.at[q, step - 1, 0], grp_rs.at[q, step - 1, 0], at_grp(to))
            )

    def finish_any(q):
        field[q] = coarse(grp, grp, q) * grp_out[q]
        for step in range(1, n_grp):
            firsts[q][step - 1].wait_recv()
            field[q] += coarse(grp, lax.rem(grp + n_grp - step, n_grp), q) * grp_in[q, step - 1]

    square = n_grp == 4

    def exchange_first():
        (start if square else start_any)(0)
        for j in range(REMOTE + 1):
            build_pick(1, j)
        if square:
            pass_on(0)
        for j in range(REMOTE + 1):
            do_meta(1, j)

    def exchange_last():
        (start if square else start_any)(1)
        for j in (REMOTE, 0):
            build_spread(1, j)
        if square:
            pass_on(1)
        for j in range(1, REMOTE):
            build_spread(1, j)
        for q in range(2):
            (finish if square else finish_any)(q)

    def nothing():
        pass

    for load in loads[2:]:
        load.wait()
    transport(0, x_ref[...], exchange_first, exchange_last)
    on_left = left((half, lev))
    whole = jnp.concatenate(
        [jnp.where(on_left, field[0], swap(field[1])), jnp.where(on_left, swap(field[0]), field[1])], axis=0
    )
    transport(1, whole, nothing, nothing)
    out_ref[...] = jnp.where(left((cols, lev)), land[0], land[1])
    for copy in sent:
        if id(copy) not in left_already:
            copy.wait_send()


def body(n_grp, n_tile, adjoint_in, departure, fraction, level_map, coarse_map):
    cols, lev = adjoint_in.shape
    half = cols // 2
    n_in = 1 if n_grp == 4 else n_grp - 1
    dma = pltpu.SemaphoreType.DMA
    return pl.pallas_call(
        functools.partial(kernel, n_grp, n_tile),
        out_shape=jax.ShapeDtypeStruct((cols, lev), F32),
        in_specs=[pl.BlockSpec(memory_space=pltpu.HBM)] * 5,
        out_specs=pl.BlockSpec(memory_space=pltpu.VMEM),
        scratch_shapes=[
            pltpu.VMEM((cols, lev), F32),
            pltpu.VMEM((2, cols), jnp.int32),
            pltpu.VMEM((2, cols), F32),
            pltpu.VMEM(level_map.shape, F32),
            pltpu.VMEM((n_grp, n_grp, lev), F32),
            pltpu.VMEM((2, 8, cols), F32),
            pltpu.VMEM((16, cols), jnp.int32),
            pltpu.VMEM((2, REMOTE + 1, half, cols), BF16),
            pltpu.VMEM((2, cols, 128), BF16),
            pltpu.VMEM((cols, 2 * lev), BF16),
            pltpu.VMEM((2, 2, REMOTE, half // 2, lev), F32),
            pltpu.VMEM((2, 2, REMOTE + 1, half // 2, lev), F32),
            pltpu.VMEM((2, REMOTE, 8, half), F32),
            pltpu.VMEM((2, REMOTE + 1, 8, half), F32),
            pltpu.VMEM((half, lev), BF16),
            pltpu.VMEM((REMOTE + 1, cols, half), BF16),
            pltpu.VMEM((REMOTE + 1, cols, half), BF16),
            pltpu.VMEM((2, cols, lev), F32),
            pltpu.VMEM((2, len(EDGE_SHIFTS) + 1, 8, lev), F32),
            pltpu.VMEM((2, len(EDGE_SHIFTS), 8, lev), F32),
            pltpu.VMEM((2, half, lev), F32),
            pltpu.VMEM((2, half, lev), F32),
            pltpu.VMEM((2, n_in, half, lev), F32),
            pltpu.VMEM((2, half, lev), F32),
            pltpu.VMEM((2, half, lev), F32),
            dma((5,)),
            dma((2, 2, REMOTE)),
            dma((2, 2, REMOTE)),
            dma((2, REMOTE)),
            dma((2, REMOTE)),
            dma((2, len(EDGE_SHIFTS))),
            dma((2, len(EDGE_SHIFTS))),
            dma((2, max(2, n_grp - 1), CHUNKS)),
            dma((2, max(2, n_grp - 1), CHUNKS)),
        ],
        compiler_params=pltpu.CompilerParams(
            collective_id=0, has_side_effects=True, vmem_limit_bytes=60 * 2 ** 20
        ),
    )(adjoint_in, departure, fraction, level_map, coarse_map.transpose(1, 2, 0))


def solution(mesh):
    return jax.shard_map(
        functools.partial(body, mesh.shape["grp"], mesh.shape["tile"]),
        mesh=mesh,
        in_specs=(
            P(("grp", "tile"), None),
            P(None, ("grp", "tile")),
            P(None, ("grp", "tile")),
            P(),
            P(),
        ),
        out_specs=P(("grp", "tile"), None),
        check_vma=False,
    )
```

```python
import functools

import jax
import jax.numpy as jnp
from jax import lax
from jax.experimental import pallas as pl
from jax.experimental.pallas import tpu as pltpu
from jax.sharding import PartitionSpec as P

REACH = 2
SHIFTS = (2, -2, 1, -1, 0)
REMOTE = 4
EDGE_SHIFTS = (1, -1, 2, -2, 3, -3)
CHUNKS = 4
ARRIVE = (2, 3, 0, 1)
BF16 = jnp.bfloat16
F32 = jnp.float32


def cubic_weights(a):
    return [
        -a * (1.0 - a) * (2.0 - a) / 6.0,
        (1.0 + a) * (1.0 - a) * (2.0 - a) / 2.0,
        (1.0 + a) * a * (2.0 - a) / 2.0,
        -(1.0 + a) * a * (1.0 - a) / 6.0,
    ]


def split(x):
    high = x.astype(BF16)
    return high, (x - high.astype(F32)).astype(BF16)


def dot(a, b):
    return jnp.dot(a, b, preferred_element_type=F32)


def dot_nt(a, b):
    return lax.dot_general(a, b, (((1,), (1,)), ((), ())), preferred_element_type=F32)


def kernel(
    n_grp, n_tile, x_hbm, dep_hbm, frac_hbm, lm_hbm, cm_hbm, out_ref,
    x_ref, dep_ref, frac_ref, lm_ref, cm_ref, meta_ref,
    slots, pick, lifted, rows_out, rows_in, meta_out, meta_in, rows_hl,
    s_high, s_low, land, edge, edge_in, field, grp_out, grp_in, grp_mid, grp_last,
    load_sem, rows_ss, rows_rs, meta_ss, meta_rs, edge_ss, edge_rs, grp_ss, grp_rs,
):
    cols, lev = x_ref.shape
    half = cols // 2
    grp = lax.axis_index("grp")
    tile = lax.axis_index("tile")

    def at_tile(by):
        return {"tile": lax.rem(tile + (by + n_tile), n_tile)}

    def at_grp(g):
        return {"grp": g}

    barrier = pltpu.get_barrier_semaphore()
    for by in EDGE_SHIFTS:
        pl.semaphore_signal(barrier, inc=1, device_id=at_tile(by), device_id_type=pl.DeviceIdType.MESH)
    for step in range(1, n_grp):
        pl.semaphore_signal(
            barrier, inc=1, device_id=at_grp(lax.rem(grp + step, n_grp)),
            device_id_type=pl.DeviceIdType.MESH,
        )
    pairs = ((dep_hbm, dep_ref), (frac_hbm, frac_ref), (x_hbm, x_ref), (lm_hbm, lm_ref), (cm_hbm, cm_ref))
    loads = [pltpu.make_async_copy(src, dst, load_sem.at[n]) for n, (src, dst) in enumerate(pairs)]
    for load in loads:
        load.start()
    for load in loads[:2]:
        load.wait()
    departure = dep_ref[...]
    target = (departure >> (cols.bit_length() - 1)) & (n_tile - 1)
    offset = ((target - tile + REACH) & (n_tile - 1)) - REACH
    values = [(departure & (cols - 1)).astype(F32)] + cubic_weights(frac_ref[...]) + [offset.astype(F32)]
    meta_ref[...] = jnp.zeros_like(meta_ref)
    for n, value in enumerate(values):
        for t in range(2):
            meta_ref[t, n : n + 1, :] = value[t : t + 1]

    sent = []
    left_already = []
    metas = ([], [])

    def send(src, dst, ss, rs, where):
        copy = pltpu.make_async_remote_copy(
            src_ref=src, dst_ref=dst, send_sem=ss, recv_sem=rs,
            device_id=where, device_id_type=pl.DeviceIdType.MESH,
        )
        copy.start()
        sent.append(copy)
        return copy

    row8 = lax.broadcasted_iota(jnp.int32, (8, cols), 0)
    wanted = jnp.full((8, cols), -100.0, F32)
    for j, by in enumerate(SHIFTS):
        wanted = jnp.where(row8 == j, float(by), wanted)
    hot = jnp.concatenate(
        [jnp.where(wanted == meta_ref[1 - t, 5:6, :], 1.0, 0.0) for t in range(2)], axis=0
    )
    lane = 128
    r = lax.broadcasted_iota(jnp.int32, (lane, 2 * lane), 0)
    c = lax.broadcasted_iota(jnp.int32, (lane, 2 * lane), 1)
    counter = jnp.where((r < c) | (c >= lane), 1.0, 0.0).astype(BF16)
    stacked = jnp.concatenate([hot[:, i * lane : (i + 1) * lane] for i in range(cols // lane)], axis=0)
    counts = dot(stacked.astype(BF16), counter)
    total = jnp.zeros((16, lane), F32)
    for i in range(cols // lane):
        own = counts[16 * i : 16 * i + 16]
        before = own[:, :lane] + total
        total = total + own[:, lane:]
        mine = hot[:, i * lane : (i + 1) * lane] > 0.5
        slots[:, i * lane : (i + 1) * lane] = jnp.where(mine, before, -1.0).astype(jnp.int32)

    block = 128

    def build_pick(t, j):
        @pl.loop(0, half // block)
        def _(i):
            r = lax.broadcasted_iota(jnp.int32, (block, lane), 0) + i * block
            at = pl.ds(pl.multiple_of(i * block, block), block)
            for n in range(0, cols, lane):
                hit = r == slots[8 * t + j : 8 * t + j + 1, n : n + lane]
                pick[t, j, at, n : n + lane] = jnp.where(hit, 1.0, 0.0).astype(BF16)

    def do_meta(t, j):
        whole = meta_ref[1 - t]
        a = whole.astype(BF16)
        rest = whole - a.astype(F32)
        parts = jnp.concatenate([a.astype(F32), rest], axis=0).astype(BF16)
        got = dot_nt(parts, pick[t, j])
        packed = got[:8] + got[8:]
        if j == REMOTE:
            meta_in[t, j] = packed
        else:
            meta_out[t, j] = packed
            metas[t].append(
                send(meta_out.at[t, j], meta_in.at[t, j], meta_ss.at[t, j], meta_rs.at[t, j], at_tile(SHIFTS[j]))
            )

    def build_spread(t, j):
        if j < REMOTE:
            metas[t][j].wait_recv()
        size = 128

        @pl.loop(0, cols // size)
        def _(i):
            cells = lax.broadcasted_iota(jnp.int32, (size, lane), 0) + i * size
            at = pl.ds(pl.multiple_of(i * size, size), size)
            for n in range(0, half, lane):
                place = meta_in[t, j, 0:1, n : n + lane].astype(jnp.int32)
                value = jnp.zeros((size, lane), F32)
                for k in range(4):
                    value = jnp.where(cells == place + (k - 1), meta_in[t, j, 1 + k : 2 + k, n : n + lane], value)
                high, low = split(value)
                s_high[j, at, n : n + lane] = high
                s_low[j, at, n : n + lane] = low

    part_lev = lev // 2

    def swap(x):
        return pltpu.roll(x, part_lev, 1)

    def left(shape):
        return lax.broadcasted_iota(jnp.int32, shape, 1) < part_lev

    def twice(x, q):
        own = x[:, q * part_lev : (q + 1) * part_lev]
        return jnp.concatenate([own, own], axis=1)

    def deposit(t, q, j, first):
        both = rows_in[t, q, j]
        high = both.astype(BF16).astype(F32)
        low = both - high
        on_left = left(both.shape)
        rows_hl[: half // 2, :] = jnp.where(on_left, high, swap(low)).astype(BF16)
        rows_hl[half // 2 :, :] = jnp.where(on_left, swap(high), low).astype(BF16)
        size = 512

        @pl.loop(0, cols // size)
        def _(i):
            at = pl.ds(pl.multiple_of(i * size, size), size)
            part = dot(s_high[j, at, :], rows_hl[...]) + dot(s_low[j, at, :], rows_hl[...])
            if first:
                land[q, at, :] = part
            else:
                land[q, at, :] += part

    def close(t, q, edges):
        land[q] = land[q] + swap(land[q])
        sums = edge[t, len(edges)]
        for n, copy in enumerate(edges):
            if q == 0:
                copy.wait_recv()
            sums = sums + edge_in[t, n]
        sums = twice(sums, q)
        r = lax.broadcasted_iota(jnp.int32, (8, lev), 0)
        land[q, 0:8, :] += jnp.where(r < 2, sums, 0.0)
        land[q, cols - 8 : cols, :] += jnp.where(r == 7, sums[2:3], 0.0)

    def send_edges(t):
        place = meta_ref[1 - t, 0:1, :]
        w = [meta_ref[1 - t, 1 + k : 2 + k, :] for k in range(4)]
        offset = meta_ref[1 - t, 5:6, :]
        last = place == float(cols - 1)
        forward = jnp.where(last, w[2], jnp.where(place == float(cols - 2), w[3], 0.0))
        forward2 = jnp.where(last, w[3], 0.0)
        backward = jnp.where(place == 0.0, w[0], 0.0)
        blocks = []
        for by in EDGE_SHIFTS + (0, 0):
            near = offset == float(by - 1)
            value = jnp.where(row8 == 0, jnp.where(near, forward, 0.0), 0.0)
            value = jnp.where(row8 == 1, jnp.where(near, forward2, 0.0), value)
            value = jnp.where(row8 == 2, jnp.where(offset == float(by + 1), backward, 0.0), value)
            blocks.append(value)
        high, low = split(jnp.concatenate(blocks, axis=0))
        wide = dot(high, lifted[...])
        sums = wide[:, :lev] + wide[:, lev:] + dot(low, lifted[:, :lev])
        copies = []
        for n, by in enumerate(EDGE_SHIFTS):
            edge[t, n] = sums[8 * n : 8 * n + 8]
            copies.append(send(edge.at[t, n], edge_in.at[t, n], edge_ss.at[t, n], edge_rs.at[t, n], at_tile(by)))
        n = len(EDGE_SHIFTS)
        edge[t, n] = sums[8 * n : 8 * n + 8]
        return copies

    def transport(t, whole, exchange_first, exchange_last):
        m_high, m_low = split(lm_ref[1 - t])
        f_high, f_low = split(whole)
        lift = dot_nt(f_high, m_high) + dot_nt(f_low, m_high) + dot_nt(f_high, m_low)
        l_high, l_low = split(lift)
        lifted[:, :lev] = l_high
        lifted[:, lev:] = l_low
        on_left = left((half // 2, lev))
        copies = ({}, {})

        def send_rows(q, j):
            copies[q][j] = (
                send(
                    rows_out.at[t, q, j], rows_in.at[t, q, j], rows_ss.at[t, q, j], rows_rs.at[t, q, j],
                    at_tile(SHIFTS[j]),
                )
            )

        for j in range(REMOTE + 1):
            if t == 0:
                build_pick(t, j)
                if j == 0:
                    pl.semaphore_wait(barrier, len(EDGE_SHIFTS) + n_grp - 1)
            both = dot(pick[t, j], lifted[...])
            packed = both[:, :lev] + both[:, lev:]
            top, bottom = packed[: half // 2], packed[half // 2 :]
            into = rows_out if j < REMOTE else rows_in
            into[t, 0, j] = jnp.where(on_left, top, swap(bottom))
            into[t, 1, j] = jnp.where(on_left, swap(top), bottom)
            if j < REMOTE:
                send_rows(0, j)
        if t == 0:
            for j in range(REMOTE + 1):
                do_meta(t, j)
        edges = send_edges(t)
        if t == 0:
            build_spread(t, REMOTE)
        for q in range(2):
            deposit(t, q, REMOTE, True)
        if t == 0:
            for j in range(REMOTE):
                build_spread(t, j)
        for j in (2, 3, 0, 1):
            copies[0][j].wait_send()
            left_already.append(id(copies[0][j]))
            send_rows(1, j)
        for q in range(2):
            for j in ARRIVE:
                copies[q][j].wait_recv()
                deposit(t, q, j, False)
            close(t, q, edges)
            (exchange_first, exchange_last)[q]()

    def coarse(b, e, q):
        return twice(cm_ref[b, pl.ds(e, 1), :], q)

    flip_x = grp + 1 - 2 * lax.rem(grp, 2)
    flip_y = lax.rem(grp + 2, n_grp)
    chunks = []
    for n in range(CHUNKS):
        near, far = ((flip_x, flip_y), (flip_y, flip_x))[n % 2]
        chunks.append((n, pl.ds(n * (half // CHUNKS), half // CHUNKS), near, far))
    firsts = ([], [])
    lasts = ([], [])

    def pack_part(q):
        grp_out[q] = jnp.where(left((half, lev)), land[q, :half, :], land[q, half:, :])

    def start(q):
        pack_part(q)
        for n, at, near, far in chunks:
            firsts[q].append(
                send(grp_out.at[q, at], grp_in.at[q, 0, at], grp_ss.at[q, 0, n], grp_rs.at[q, 0, n], at_grp(near))
            )

    def pass_on(q):
        for n, at, near, far in chunks:
            firsts[q][n].wait_recv()
            grp_mid[q, at, :] = coarse(far, grp, q) * grp_out[q, at, :] + coarse(far, near, q) * grp_in[q, 0, at, :]
            lasts[q].append(
                send(grp_mid.at[q, at], grp_last.at[q, at], grp_ss.at[q, 1, n], grp_rs.at[q, 1, n], at_grp(far))
            )
        for n, at, near, far in chunks:
            field[q, at, :] = coarse(grp, grp, q) * grp_out[q, at, :] + coarse(grp, near, q) * grp_in[q, 0, at, :]

    def finish(q):
        for n, at, near, far in chunks:
            lasts[q][n].wait_recv()
            field[q, at, :] += grp_last[q, at, :]

    def start_any(q):
        pack_part(q)
        for step in range(1, n_grp):
            to = lax.rem(grp + step, n_grp)
            firsts[q].append(
                send(grp_out.at[q], grp_in.at[q, step - 1], grp_ss.at[q, step - 1, 0], grp_rs.at[q, step - 1, 0], at_grp(to))
            )

    def finish_any(q):
        field[q] = coarse(grp, grp, q) * grp_out[q]
        for step in range(1, n_grp):
            firsts[q][step - 1].wait_recv()
            field[q] += coarse(grp, lax.rem(grp + n_grp - step, n_grp), q) * grp_in[q, step - 1]

    square = n_grp == 4

    def exchange_first():
        (start if square else start_any)(0)
        for j in range(REMOTE + 1):
            build_pick(1, j)
        if square:
            pass_on(0)
        for j in range(REMOTE + 1):
            do_meta(1, j)

    def exchange_last():
        (start if square else start_any)(1)
        for j in (REMOTE, 0):
            build_spread(1, j)
        if square:
            pass_on(1)
        for j in range(1, REMOTE):
            build_spread(1, j)
        for q in range(2):
            (finish if square else finish_any)(q)

    def nothing():
        pass

    for load in loads[2:]:
        load.wait()
    transport(0, x_ref[...], exchange_first, exchange_last)
    on_left = left((half, lev))
    whole = jnp.concatenate(
        [jnp.where(on_left, field[0], swap(field[1])), jnp.where(on_left, swap(field[0]), field[1])], axis=0
    )
    transport(1, whole, nothing, nothing)
    out_ref[...] = jnp.where(left((cols, lev)), land[0], land[1])
    for copy in sent:
        if id(copy) not in left_already:
            copy.wait_send()


def body(n_grp, n_tile, adjoint_in, departure, fraction, level_map, coarse_map):
    cols, lev = adjoint_in.shape
    half = cols // 2
    n_in = 1 if n_grp == 4 else n_grp - 1
    dma = pltpu.SemaphoreType.DMA
    return pl.pallas_call(
        functools.partial(kernel, n_grp, n_tile),
        out_shape=jax.ShapeDtypeStruct((cols, lev), F32),
        in_specs=[pl.BlockSpec(memory_space=pltpu.HBM)] * 5,
        out_specs=pl.BlockSpec(memory_space=pltpu.VMEM),
        scratch_shapes=[
            pltpu.VMEM((cols, lev), F32),
            pltpu.VMEM((2, cols), jnp.int32),
            pltpu.VMEM((2, cols), F32),
            pltpu.VMEM(level_map.shape, F32),
            pltpu.VMEM((n_grp, n_grp, lev), F32),
            pltpu.VMEM((2, 8, cols), F32),
            pltpu.VMEM((16, cols), jnp.int32),
            pltpu.VMEM((2, REMOTE + 1, half, cols), BF16),
            pltpu.VMEM((cols, 2 * lev), BF16),
            pltpu.VMEM((2, 2, REMOTE, half // 2, lev), F32),
            pltpu.VMEM((2, 2, REMOTE + 1, half // 2, lev), F32),
            pltpu.VMEM((2, REMOTE, 8, half), F32),
            pltpu.VMEM((2, REMOTE + 1, 8, half), F32),
            pltpu.VMEM((half, lev), BF16),
            pltpu.VMEM((REMOTE + 1, cols, half), BF16),
            pltpu.VMEM((REMOTE + 1, cols, half), BF16),
            pltpu.VMEM((2, cols, lev), F32),
            pltpu.VMEM((2, len(EDGE_SHIFTS) + 1, 8, lev), F32),
            pltpu.VMEM((2, len(EDGE_SHIFTS), 8, lev), F32),
            pltpu.VMEM((2, half, lev), F32),
            pltpu.VMEM((2, half, lev), F32),
            pltpu.VMEM((2, n_in, half, lev), F32),
            pltpu.VMEM((2, half, lev), F32),
            pltpu.VMEM((2, half, lev), F32),
            dma((5,)),
            dma((2, 2, REMOTE)),
            dma((2, 2, REMOTE)),
            dma((2, REMOTE)),
            dma((2, REMOTE)),
            dma((2, len(EDGE_SHIFTS))),
            dma((2, len(EDGE_SHIFTS))),
            dma((2, max(2, n_grp - 1), CHUNKS)),
            dma((2, max(2, n_grp - 1), CHUNKS)),
        ],
        compiler_params=pltpu.CompilerParams(
            collective_id=0, has_side_effects=True, vmem_limit_bytes=60 * 2 ** 20
        ),
    )(adjoint_in, departure, fraction, level_map, coarse_map.transpose(1, 2, 0))


def solution(mesh):
    return jax.shard_map(
        functools.partial(body, mesh.shape["grp"], mesh.shape["tile"]),
        mesh=mesh,
        in_specs=(
            P(("grp", "tile"), None),
            P(None, ("grp", "tile")),
            P(None, ("grp", "tile")),
            P(),
            P(),
        ),
        out_specs=P(("grp", "tile"), None),
        check_vma=False,
    )
```

```python
import functools

import jax
import jax.numpy as jnp
from jax import lax
from jax.experimental import pallas as pl
from jax.experimental.pallas import tpu as pltpu
from jax.sharding import PartitionSpec as P

REACH = 2
SHIFTS = (2, -2, 1, -1, 0)
REMOTE = 4
EDGE_SHIFTS = (1, -1, 2, -2, 3, -3)
CHUNKS = 4
ARRIVE = (2, 3, 0, 1)
BF16 = jnp.bfloat16
F32 = jnp.float32


def cubic_weights(a):
    return [
        -a * (1.0 - a) * (2.0 - a) / 6.0,
        (1.0 + a) * (1.0 - a) * (2.0 - a) / 2.0,
        (1.0 + a) * a * (2.0 - a) / 2.0,
        -(1.0 + a) * a * (1.0 - a) / 6.0,
    ]


def split(x):
    high = x.astype(BF16)
    return high, (x - high.astype(F32)).astype(BF16)


def dot(a, b):
    return jnp.dot(a, b, preferred_element_type=F32)


def dot_nt(a, b):
    return lax.dot_general(a, b, (((1,), (1,)), ((), ())), preferred_element_type=F32)


def kernel(
    n_grp, n_tile, x_hbm, dep_hbm, frac_hbm, lm_hbm, cm_hbm, out_ref,
    x_ref, dep_ref, frac_ref, lm_ref, cm_ref, meta_ref,
    slots, pick, lifted, rows_out, rows_in, meta_out, meta_in, rows_hl,
    s_high, s_low, land, edge, edge_in, field, grp_out, grp_in, grp_mid, grp_last,
    load_sem, rows_ss, rows_rs, meta_ss, meta_rs, edge_ss, edge_rs, grp_ss, grp_rs,
):
    cols, lev = x_ref.shape
    half = cols // 2
    grp = lax.axis_index("grp")
    tile = lax.axis_index("tile")

    def at_tile(by):
        return {"tile": lax.rem(tile + (by + n_tile), n_tile)}

    def at_grp(g):
        return {"grp": g}

    barrier = pltpu.get_barrier_semaphore()
    for by in EDGE_SHIFTS:
        pl.semaphore_signal(barrier, inc=1, device_id=at_tile(by), device_id_type=pl.DeviceIdType.MESH)
    for step in range(1, n_grp):
        pl.semaphore_signal(
            barrier, inc=1, device_id=at_grp(lax.rem(grp + step, n_grp)),
            device_id_type=pl.DeviceIdType.MESH,
        )
    pairs = ((dep_hbm, dep_ref), (frac_hbm, frac_ref), (x_hbm, x_ref), (lm_hbm, lm_ref), (cm_hbm, cm_ref))
    loads = [pltpu.make_async_copy(src, dst, load_sem.at[n]) for n, (src, dst) in enumerate(pairs)]
    for load in loads:
        load.start()
    for load in loads[:2]:
        load.wait()
    departure = dep_ref[...]
    target = (departure >> (cols.bit_length() - 1)) & (n_tile - 1)
    offset = ((target - tile + REACH) & (n_tile - 1)) - REACH
    values = [(departure & (cols - 1)).astype(F32)] + cubic_weights(frac_ref[...]) + [offset.astype(F32)]
    meta_ref[...] = jnp.zeros_like(meta_ref)
    for n, value in enumerate(values):
        for t in range(2):
            meta_ref[t, n : n + 1, :] = value[t : t + 1]

    sent = []
    left_already = []
    metas = ([], [])

    def send(src, dst, ss, rs, where):
        copy = pltpu.make_async_remote_copy(
            src_ref=src, dst_ref=dst, send_sem=ss, recv_sem=rs,
            device_id=where, device_id_type=pl.DeviceIdType.MESH,
        )
        copy.start()
        sent.append(copy)
        return copy

    row8 = lax.broadcasted_iota(jnp.int32, (8, cols), 0)
    wanted = jnp.full((8, cols), -100.0, F32)
    for j, by in enumerate(SHIFTS):
        wanted = jnp.where(row8 == j, float(by), wanted)
    hot = jnp.concatenate(
        [jnp.where(wanted == meta_ref[1 - t, 5:6, :], 1.0, 0.0) for t in range(2)], axis=0
    )
    lane = 128
    r = lax.broadcasted_iota(jnp.int32, (lane, 2 * lane), 0)
    c = lax.broadcasted_iota(jnp.int32, (lane, 2 * lane), 1)
    counter = jnp.where((r < c) | (c >= lane), 1.0, 0.0).astype(BF16)
    stacked = jnp.concatenate([hot[:, i * lane : (i + 1) * lane] for i in range(cols // lane)], axis=0)
    counts = dot(stacked.astype(BF16), counter)
    total = jnp.zeros((16, lane), F32)
    for i in range(cols // lane):
        own = counts[16 * i : 16 * i + 16]
        before = own[:, :lane] + total
        total = total + own[:, lane:]
        mine = hot[:, i * lane : (i + 1) * lane] > 0.5
        slots[:, i * lane : (i + 1) * lane] = jnp.where(mine, before, -1.0).astype(jnp.int32)

    block = 128

    def build_pick(t, j):
        @pl.loop(0, half // block)
        def _(i):
            r = lax.broadcasted_iota(jnp.int32, (block, cols), 0) + i * block
            hit = r == slots[8 * t + j : 8 * t + j + 1, :]
            pick[t, j, pl.ds(pl.multiple_of(i * block, block), block), :] = jnp.where(hit, 1.0, 0.0).astype(BF16)

    def do_meta(t, j):
        whole = meta_ref[1 - t]
        a = whole.astype(BF16)
        rest = whole - a.astype(F32)
        parts = jnp.concatenate([a.astype(F32), rest], axis=0).astype(BF16)
        got = dot_nt(parts, pick[t, j])
        packed = got[:8] + got[8:]
        if j == REMOTE:
            meta_in[t, j] = packed
        else:
            meta_out[t, j] = packed
            metas[t].append(
                send(meta_out.at[t, j], meta_in.at[t, j], meta_ss.at[t, j], meta_rs.at[t, j], at_tile(SHIFTS[j]))
            )

    def build_spread(t, j):
        if j < REMOTE:
            metas[t][j].wait_recv()
        size = 128

        @pl.loop(0, cols // size)
        def _(i):
            cells = lax.broadcasted_iota(jnp.int32, (size, half), 0) + i * size
            place = meta_in[t, j, 0:1, :].astype(jnp.int32)
            value = jnp.zeros((size, half), F32)
            for k in range(4):
                value = jnp.where(cells == place + (k - 1), meta_in[t, j, 1 + k : 2 + k, :], value)
            high, low = split(value)
            at = pl.ds(pl.multiple_of(i * size, size), size)
            s_high[j, at, :] = high
            s_low[j, at, :] = low

    part_lev = lev // 2

    def swap(x):
        return pltpu.roll(x, part_lev, 1)

    def left(shape):
        return lax.broadcasted_iota(jnp.int32, shape, 1) < part_lev

    def twice(x, q):
        own = x[:, q * part_lev : (q + 1) * part_lev]
        return jnp.concatenate([own, own], axis=1)

    def deposit(t, q, j, first):
        both = rows_in[t, q, j]
        high = both.astype(BF16).astype(F32)
        low = both - high
        on_left = left(both.shape)
        rows_hl[: half // 2, :] = jnp.where(on_left, high, swap(low)).astype(BF16)
        rows_hl[half // 2 :, :] = jnp.where(on_left, swap(high), low).astype(BF16)
        size = 512

        @pl.loop(0, cols // size)
        def _(i):
            at = pl.ds(pl.multiple_of(i * size, size), size)
            part = dot(s_high[j, at, :], rows_hl[...]) + dot(s_low[j, at, :], rows_hl[...])
            if first:
                land[q, at, :] = part
            else:
                land[q, at, :] += part

    def close(t, q, edges):
        land[q] = land[q] + swap(land[q])
        sums = edge[t, len(edges)]
        for n, copy in enumerate(edges):
            if q == 0:
                copy.wait_recv()
            sums = sums + edge_in[t, n]
        sums = twice(sums, q)
        r = lax.broadcasted_iota(jnp.int32, (8, lev), 0)
        land[q, 0:8, :] += jnp.where(r < 2, sums, 0.0)
        land[q, cols - 8 : cols, :] += jnp.where(r == 7, sums[2:3], 0.0)

    def send_edges(t):
        place = meta_ref[1 - t, 0:1, :]
        w = [meta_ref[1 - t, 1 + k : 2 + k, :] for k in range(4)]
        offset = meta_ref[1 - t, 5:6, :]
        last = place == float(cols - 1)
        forward = jnp.where(last, w[2], jnp.where(place == float(cols - 2), w[3], 0.0))
        forward2 = jnp.where(last, w[3], 0.0)
        backward = jnp.where(place == 0.0, w[0], 0.0)
        blocks = []
        for by in EDGE_SHIFTS + (0, 0):
            near = offset == float(by - 1)
            value = jnp.where(row8 == 0, jnp.where(near, forward, 0.0), 0.0)
            value = jnp.where(row8 == 1, jnp.where(near, forward2, 0.0), value)
            value = jnp.where(row8 == 2, jnp.where(offset == float(by + 1), backward, 0.0), value)
            blocks.append(value)
        high, low = split(jnp.concatenate(blocks, axis=0))
        wide = dot(high, lifted[...])
        sums = wide[:, :lev] + wide[:, lev:] + dot(low, lifted[:, :lev])
        copies = []
        for n, by in enumerate(EDGE_SHIFTS):
            edge[t, n] = sums[8 * n : 8 * n + 8]
            copies.append(send(edge.at[t, n], edge_in.at[t, n], edge_ss.at[t, n], edge_rs.at[t, n], at_tile(by)))
        n = len(EDGE_SHIFTS)
        edge[t, n] = sums[8 * n : 8 * n + 8]
        return copies

    def transport(t, whole, exchange_first, exchange_last):
        m_high, m_low = split(lm_ref[1 - t])
        f_high, f_low = split(whole)
        lift = dot_nt(f_high, m_high) + dot_nt(f_low, m_high) + dot_nt(f_high, m_low)
        l_high, l_low = split(lift)
        lifted[:, :lev] = l_high
        lifted[:, lev:] = l_low
        on_left = left((half // 2, lev))
        copies = ({}, {})

        def send_rows(q, j):
            copies[q][j] = (
                send(
                    rows_out.at[t, q, j], rows_in.at[t, q, j], rows_ss.at[t, q, j], rows_rs.at[t, q, j],
                    at_tile(SHIFTS[j]),
                )
            )

        for j in range(REMOTE + 1):
            if t == 0:
                build_pick(t, j)
                if j == 0:
                    pl.semaphore_wait(barrier, len(EDGE_SHIFTS) + n_grp - 1)
            both = dot(pick[t, j], lifted[...])
            packed = both[:, :lev] + both[:, lev:]
            top, bottom = packed[: half // 2], packed[half // 2 :]
            into = rows_out if j < REMOTE else rows_in
            into[t, 0, j] = jnp.where(on_left, top, swap(bottom))
            into[t, 1, j] = jnp.where(on_left, swap(top), bottom)
            if j < REMOTE:
                send_rows(0, j)
        if t == 0:
            for j in range(REMOTE + 1):
                do_meta(t, j)
        edges = send_edges(t)
        if t == 0:
            build_spread(t, REMOTE)
        for q in range(2):
            deposit(t, q, REMOTE, True)
        for j in (2, 3, 0, 1):
            copies[0][j].wait_send()
            left_already.append(id(copies[0][j]))
            send_rows(1, j)
            if t == 0:
                build_spread(t, j)
        for q in range(2):
            for j in ARRIVE:
                copies[q][j].wait_recv()
                deposit(t, q, j, False)
            close(t, q, edges)
            (exchange_first, exchange_last)[q]()

    def coarse(b, e, q):
        return twice(cm_ref[b, pl.ds(e, 1), :], q)

    flip_x = grp + 1 - 2 * lax.rem(grp, 2)
    flip_y = lax.rem(grp + 2, n_grp)
    chunks = []
    for n in range(CHUNKS):
        near, far = ((flip_x, flip_y), (flip_y, flip_x))[n % 2]
        chunks.append((n, pl.ds(n * (half // CHUNKS), half // CHUNKS), near, far))
    firsts = ([], [])
    lasts = ([], [])

    def pack_part(q):
        grp_out[q] = jnp.where(left((half, lev)), land[q, :half, :], land[q, half:, :])

    def start(q):
        pack_part(q)
        for n, at, near, far in chunks:
            firsts[q].append(
                send(grp_out.at[q, at], grp_in.at[q, 0, at], grp_ss.at[q, 0, n], grp_rs.at[q, 0, n], at_grp(near))
            )

    def pass_on(q):
        for n, at, near, far in chunks:
            firsts[q][n].wait_recv()
            grp_mid[q, at, :] = coarse(far, grp, q) * grp_out[q, at, :] + coarse(far, near, q) * grp_in[q, 0, at, :]
            lasts[q].append(
                send(grp_mid.at[q, at], grp_last.at[q, at], grp_ss.at[q, 1, n], grp_rs.at[q, 1, n], at_grp(far))
            )
        for n, at, near, far in chunks:
            field[q, at, :] = coarse(grp, grp, q) * grp_out[q, at, :] + coarse(grp, near, q) * grp_in[q, 0, at, :]

    def finish(q):
        for n, at, near, far in chunks:
            lasts[q][n].wait_recv()
            field[q, at, :] += grp_last[q, at, :]

    def start_any(q):
        pack_part(q)
        for step in range(1, n_grp):
            to = lax.rem(grp + step, n_grp)
            firsts[q].append(
                send(grp_out.at[q], grp_in.at[q, step - 1], grp_ss.at[q, step - 1, 0], grp_rs.at[q, step - 1, 0], at_grp(to))
            )

    def finish_any(q):
        field[q] = coarse(grp, grp, q) * grp_out[q]
        for step in range(1, n_grp):
            firsts[q][step - 1].wait_recv()
            field[q] += coarse(grp, lax.rem(grp + n_grp - step, n_grp), q) * grp_in[q, step - 1]

    square = n_grp == 4

    def exchange_first():
        (start if square else start_any)(0)
        for j in range(REMOTE + 1):
            build_pick(1, j)
        if square:
            pass_on(0)
        for j in range(REMOTE + 1):
            do_meta(1, j)

    def exchange_last():
        (start if square else start_any)(1)
        for j in (REMOTE, 0):
            build_spread(1, j)
        if square:
            pass_on(1)
        for j in range(1, REMOTE):
            build_spread(1, j)
        for q in range(2):
            (finish if square else finish_any)(q)

    def nothing():
        pass

    for load in loads[2:]:
        load.wait()
    transport(0, x_ref[...], exchange_first, exchange_last)
    on_left = left((half, lev))
    whole = jnp.concatenate(
        [jnp.where(on_left, field[0], swap(field[1])), jnp.where(on_left, swap(field[0]), field[1])], axis=0
    )
    transport(1, whole, nothing, nothing)
    out_ref[...] = jnp.where(left((cols, lev)), land[0], land[1])
    for copy in sent:
        if id(copy) not in left_already:
            copy.wait_send()


def body(n_grp, n_tile, adjoint_in, departure, fraction, level_map, coarse_map):
    cols, lev = adjoint_in.shape
    half = cols // 2
    n_in = 1 if n_grp == 4 else n_grp - 1
    dma = pltpu.SemaphoreType.DMA
    return pl.pallas_call(
        functools.partial(kernel, n_grp, n_tile),
        out_shape=jax.ShapeDtypeStruct((cols, lev), F32),
        in_specs=[pl.BlockSpec(memory_space=pltpu.HBM)] * 5,
        out_specs=pl.BlockSpec(memory_space=pltpu.VMEM),
        scratch_shapes=[
            pltpu.VMEM((cols, lev), F32),
            pltpu.VMEM((2, cols), jnp.int32),
            pltpu.VMEM((2, cols), F32),
            pltpu.VMEM(level_map.shape, F32),
            pltpu.VMEM((n_grp, n_grp, lev), F32),
            pltpu.VMEM((2, 8, cols), F32),
            pltpu.VMEM((16, cols), jnp.int32),
            pltpu.VMEM((2, REMOTE + 1, half, cols), BF16),
            pltpu.VMEM((cols, 2 * lev), BF16),
            pltpu.VMEM((2, 2, REMOTE, half // 2, lev), F32),
            pltpu.VMEM((2, 2, REMOTE + 1, half // 2, lev), F32),
            pltpu.VMEM((2, REMOTE, 8, half), F32),
            pltpu.VMEM((2, REMOTE + 1, 8, half), F32),
            pltpu.VMEM((half, lev), BF16),
            pltpu.VMEM((REMOTE + 1, cols, half), BF16),
            pltpu.VMEM((REMOTE + 1, cols, half), BF16),
            pltpu.VMEM((2, cols, lev), F32),
            pltpu.VMEM((2, len(EDGE_SHIFTS) + 1, 8, lev), F32),
            pltpu.VMEM((2, len(EDGE_SHIFTS), 8, lev), F32),
            pltpu.VMEM((2, half, lev), F32),
            pltpu.VMEM((2, half, lev), F32),
            pltpu.VMEM((2, n_in, half, lev), F32),
            pltpu.VMEM((2, half, lev), F32),
            pltpu.VMEM((2, half, lev), F32),
            dma((5,)),
            dma((2, 2, REMOTE)),
            dma((2, 2, REMOTE)),
            dma((2, REMOTE)),
            dma((2, REMOTE)),
            dma((2, len(EDGE_SHIFTS))),
            dma((2, len(EDGE_SHIFTS))),
            dma((2, max(2, n_grp - 1), CHUNKS)),
            dma((2, max(2, n_grp - 1), CHUNKS)),
        ],
        compiler_params=pltpu.CompilerParams(
            collective_id=0, has_side_effects=True, vmem_limit_bytes=60 * 2 ** 20
        ),
    )(adjoint_in, departure, fraction, level_map, coarse_map.transpose(1, 2, 0))


def solution(mesh):
    return jax.shard_map(
        functools.partial(body, mesh.shape["grp"], mesh.shape["tile"]),
        mesh=mesh,
        in_specs=(
            P(("grp", "tile"), None),
            P(None, ("grp", "tile")),
            P(None, ("grp", "tile")),
            P(),
            P(),
        ),
        out_specs=P(("grp", "tile"), None),
        check_vma=False,
    )
```
